32 devices in a mesh: seq: 8 (over z, y), fsdp: 4 (over x, core).
Axes of the slice: x: 2, y: 2, z: 4, core: 2. Of those that a mesh axis runs over, the one named last changes fastest.
Arguments:
- queries: bfloat16 [4096, 64, 128], P('seq', 'fsdp'), may hold values from -8 to 8
- key_states: bfloat16 [4096, 8, 128], P('seq', 'fsdp'), may hold values from -8 to 8
- value_states: bfloat16 [4096, 8, 128], P('seq', 'fsdp'), may hold values from -6 to 6
- grad_output: bfloat16 [4096, 64, 128], P('seq', 'fsdp'), may hold values from -15 to 15
- parents: int32 [32], replicated, may hold values from -1 to 30, as said below
- projection: bfloat16 [8, 256, 5120], P(None, 'seq', 'fsdp'), may hold values from -0.078125 to 0.078125
Outputs:
- grad_queries: bfloat16 [4096, 64, 128], P('seq', 'fsdp')
- grad_keys: bfloat16 [4096, 8, 128], P('seq', 'fsdp')
- grad_values: bfloat16 [4096, 8, 128], P('seq', 'fsdp')
- grad_inputs: bfloat16 [4096, 5120], P('seq', 'fsdp')
The draws below stay inside these ranges and needn't reach their ends.
Inputs may be any that keep to these rules, and one draw needn't show every extreme that they name: `parents`: each tree is 16 consecutive blocks. Its first block has parent -1; its blocks 1 to 4 - 1 (the shared prompt) each continue the block before; its last block continues the block before it; every other later block continues an earlier block of the same tree, numbered 4 - 1 or higher within the tree.
All inputs are finite; a program needn't handle non-finite values.
Results may differ from the reference program's by a relative error of at most 0.015.
Values may be sent and summed in bfloat16 or wider, within the bound.
No kernel may reach another device: no remote copies, remote signals or barrier semaphores. Data moves between devices by JAX's collectives and lax.ppermute only.
A program may use at most 128 MiB of HBM per device.

```python
import math
import jax
import jax.numpy as jnp
from jax import lax

HEADS = 64
KVH = 8
HD = 128
D = 5120
BLK = 128
BLK_DEV = 4
SPAN = 4
NBLK = 32
TOKENS = 4096


def draw_queries(key, part):
    key = jax.random.fold_in(key, 1)
    shape = (TOKENS, HEADS, HD)
    drawn = jnp.clip(jax.random.normal(key, shape, jnp.float32), -8.0, 8.0)
    return drawn.astype(jnp.bfloat16)


def draw_key_states(key, part):
    key = jax.random.fold_in(key, 2)
    shape = (TOKENS, KVH, HD)
    drawn = jnp.clip(jax.random.normal(key, shape, jnp.float32), -8.0, 8.0)
    return drawn.astype(jnp.bfloat16)


def draw_parents(key, part):
    key = jax.random.fold_in(key, 3)
    tree_blocks = SPAN * BLK_DEV
    block_index = jnp.arange(NBLK, dtype=jnp.int32)
    local_index = block_index % tree_blocks
    tree_start = block_index - local_index
    random_pick = jax.random.randint(key, (NBLK,), 0, 1 << 20, dtype=jnp.int32)
    choices_here = jnp.maximum(local_index - BLK_DEV + 1, 1)
    branch_parent = BLK_DEV - 1 + random_pick % choices_here
    chain_parent = local_index - 1
    parent_local = jnp.where(local_index < BLK_DEV, chain_parent, branch_parent)
    parent_local = jnp.where(local_index == tree_blocks - 1, chain_parent, parent_local)
    return jnp.where(local_index == 0, -1, tree_start + parent_local).astype(jnp.int32)


def level_of(own_key, shape, pieces, smallest, high):
    def one(dim, blocks):
        heights = jax.random.uniform(jax.random.fold_in(jax.random.fold_in(own_key, 6), dim), (blocks,), jnp.float32, smallest / len(pieces), high / len(pieces))
        return jnp.repeat(jnp.exp(heights), shape[dim] // blocks).reshape((-1,) + (1,) * (len(shape) - dim - 1))

    gain = one(*pieces[0])
    for cut in pieces[1:]:
        gain = gain * one(*cut)
    return gain


def noise(own_key, shape, spread, bound, shards=(), kind=jnp.bfloat16):
    array = spread * jax.random.normal(own_key, shape, jnp.float32)
    if shards:
        array = array * level_of(own_key, shape, shards, -0.22, 0.18)
    return jnp.clip(array, -bound, bound).astype(kind)


def setup_inputs(seed: int = 0) -> dict:
    streams_of = jax.random.split(jax.random.key(seed), 7)
    queries = draw_queries(jax.random.fold_in(streams_of[6], 71), 0)
    key_states = draw_key_states(jax.random.fold_in(streams_of[6], 71), 0)
    value_states = noise(streams_of[2], (TOKENS, KVH, HD), 1.0, 6.0, ((0, 8), (1, 4)))
    grad_output = noise(streams_of[3], (TOKENS, HEADS, HD), 2.5, 15.0, ((0, 8), (1, 4)))
    parents = draw_parents(jax.random.fold_in(streams_of[6], 71), 0)
    projection = noise(streams_of[5], (KVH, 2 * HD, D), D ** -0.5, 0.078125, ((1, 8), (2, 4)))
    return dict(queries=queries, key_states=key_states, value_states=value_states, grad_output=grad_output, parents=parents, projection=projection)


def ancestors(parents, blocks, candidates, depth):

    def advance(round_index, carry):
        current, marked = carry
        matched = (candidates[None, :] == current[:, None]) & (current[:, None] >= 0)
        marked = marked | matched
        parent_now = jnp.where(current >= 0, parents[jnp.maximum(current, 0)], -1)
        return (parent_now.astype(jnp.int32), marked)
    marked = jnp.zeros((blocks.shape[0], candidates.shape[0]), bool)
    return lax.fori_loop(0, depth, advance, (blocks.astype(jnp.int32), marked))[1]

def token_mask(ancestry, query_glob, key_glob, block_len):
    expanded = jnp.repeat(jnp.repeat(ancestry, block_len, axis=0), block_len, axis=1)
    query_block = query_glob // block_len
    key_block = key_glob // block_len
    ordered = (key_block[None, :] != query_block[:, None]) | (key_glob[None, :] <= query_glob[:, None])
    return expanded & ordered

def head_backward(query_head, grad_head, key_head, value_head, visible, score_scale):
    scores = score_scale * jnp.dot(query_head, key_head.T, preferred_element_type=jnp.float32)
    scores = jnp.where(visible, scores, -jnp.inf)
    row_max = lax.optimization_barrier(jnp.max(scores, axis=1, keepdims=True))
    probs = jnp.exp(scores - row_max)
    probs = probs / lax.optimization_barrier(jnp.sum(probs, axis=1, keepdims=True))
    probs_low = probs.astype(jnp.bfloat16)
    grad_prob = jnp.dot(grad_head, value_head.T, preferred_element_type=jnp.float32)
    row_dot = lax.optimization_barrier(jnp.sum(probs * grad_prob, axis=1, keepdims=True))
    grad_score = (probs * (grad_prob - row_dot)).astype(jnp.bfloat16)
    grad_query = score_scale * jnp.dot(grad_score, key_head, preferred_element_type=jnp.float32)
    grad_key = score_scale * jnp.dot(grad_score.T, query_head, preferred_element_type=jnp.float32)
    grad_value = jnp.dot(probs_low.T, grad_head, preferred_element_type=jnp.float32)
    return (grad_query, grad_key, grad_value)

def reference(queries, key_states, value_states, grad_output, parents, projection):
    tree_blocks = SPAN * BLK_DEV
    tree_tokens = tree_blocks * BLK
    tree_count = NBLK // tree_blocks
    group_size = HEADS // KVH
    score_scale = 1.0 / math.sqrt(HD)

    def one_tree(tree_index):
        first_token = tree_index * tree_tokens
        tree_queries = lax.dynamic_slice_in_dim(queries, first_token, tree_tokens, 0)
        tree_keys = lax.dynamic_slice_in_dim(key_states, first_token, tree_tokens, 0)
        tree_values = lax.dynamic_slice_in_dim(value_states, first_token, tree_tokens, 0)
        tree_grads = lax.dynamic_slice_in_dim(grad_output, first_token, tree_tokens, 0)
        blocks = (tree_index * tree_blocks + jnp.arange(tree_blocks, dtype=jnp.int32)).astype(jnp.int32)
        ancestry = ancestors(parents, blocks, blocks, tree_blocks)
        glob = (first_token + jnp.arange(tree_tokens, dtype=jnp.int32)).astype(jnp.int32)
        visible = token_mask(ancestry, glob, glob, BLK)

        def one_pair(shared_head):
            key_head = lax.dynamic_index_in_dim(tree_keys, shared_head, 1, keepdims=False)
            value_head = lax.dynamic_index_in_dim(tree_values, shared_head, 1, keepdims=False)

            def one_query(member):
                head_index = shared_head * group_size + member
                query_head = lax.dynamic_index_in_dim(tree_queries, head_index, 1, keepdims=False)
                grad_head = lax.dynamic_index_in_dim(tree_grads, head_index, 1, keepdims=False)
                grad_query, grad_key, grad_value = head_backward(query_head, grad_head, key_head, value_head, visible, score_scale)
                return (grad_query.astype(jnp.bfloat16), grad_key, grad_value)
            grad_query, grad_key, grad_value = lax.map(one_query, jnp.arange(group_size, dtype=jnp.int32))
            return (grad_query, lax.optimization_barrier(jnp.sum(grad_key, axis=0)).astype(jnp.bfloat16), lax.optimization_barrier(jnp.sum(grad_value, axis=0)).astype(jnp.bfloat16))
        grad_query, grad_key, grad_value = lax.map(one_pair, jnp.arange(KVH, dtype=jnp.int32))
        grad_query = jnp.transpose(grad_query.reshape(HEADS, tree_tokens, HD), (1, 0, 2))
        return (grad_query, jnp.transpose(grad_key, (1, 0, 2)), jnp.transpose(grad_value, (1, 0, 2)))
    grad_queries, grad_keys, grad_values = lax.map(one_tree, jnp.arange(tree_count, dtype=jnp.int32))
    grad_queries = grad_queries.reshape(TOKENS, HEADS, HD)
    grad_keys = grad_keys.reshape(TOKENS, KVH, HD)
    grad_values = grad_values.reshape(TOKENS, KVH, HD)
    pair_grads = jnp.concatenate([grad_keys, grad_values], axis=2)

    def add_head(head_index, running):
        grad_head = lax.dynamic_index_in_dim(pair_grads, head_index, 1, keepdims=False)
        weight_head = lax.dynamic_index_in_dim(projection, head_index, 0, keepdims=False)
        term = jnp.dot(grad_head, weight_head, preferred_element_type=jnp.float32)
        rounded = lax.optimization_barrier(term.astype(jnp.bfloat16))
        return running + rounded.astype(jnp.float32)
    grad_inputs = lax.fori_loop(0, KVH, add_head, jnp.zeros((TOKENS, D), jnp.float32)).astype(jnp.bfloat16)
    return (grad_queries, grad_keys, grad_values, grad_inputs)
```

```python
import functools
import math

import jax
import jax.numpy as jnp
from jax import lax
from jax.experimental import pallas as pl
from jax.experimental.pallas import tpu as pltpu
from jax.sharding import PartitionSpec as P

BLK = 128
SPAN = 4
NEG = -1e30
LOG2E = 1.4426950408889634

NT = (((1,), (1,)), ((), ()))
TN = (((0,), (0,)), ((), ()))
NN = (((1,), (0,)), ((), ()))


def dot(a, b, dims):
    return lax.dot_general(a, b, dims, preferred_element_type=jnp.float32)


def attention_kernel(
    parents_ref, pos_ref, q_ref, g_ref, *refs, group, head_dim, blocks_here, scale
):
    kv_refs = refs[:SPAN]
    dq_ref, own_ref = refs[SPAN : SPAN + 2]
    far_refs = refs[SPAN + 2 : 2 * SPAN + 1]
    kwin, vwin, dk, dv, sbuf, gbuf, path = refs[2 * SPAN + 1 :]
    step = pl.program_id(0)
    tokens = blocks_here * BLK
    lanes = group * BLK
    factor = scale * LOG2E

    @pl.when(step == 0)
    def _():
        for offset in range(SPAN):
            rows = pl.ds((SPAN - 1 - offset) * tokens, tokens)
            kwin[rows, :] = kv_refs[offset][:, :head_dim]
            vwin[rows, :] = kv_refs[offset][:, head_dim:]
        dk[...] = jnp.zeros_like(dk)
        dv[...] = jnp.zeros_like(dv)

    pos = pos_ref[0]
    first = (pos - (SPAN - 1)) * blocks_here
    own = pos * blocks_here + step

    def walk(carry):
        current, count = carry
        path[count] = current - first
        return parents_ref[current], count + 1

    count = lax.while_loop(lambda c: c[0] >= 0, walk, (own, jnp.int32(0)))[1]

    def rows_of(k):
        return pl.ds(pl.multiple_of(path[k] * BLK, BLK), BLK)

    q = q_ref[...].reshape(lanes, head_dim)
    g = g_ref[...].reshape(lanes, head_dim)

    s = dot(kwin[rows_of(0), :], q, NT)
    key = lax.broadcasted_iota(jnp.int32, (BLK, lanes), 0)
    query = lax.broadcasted_iota(jnp.int32, (BLK, lanes), 1) & (BLK - 1)
    s = jnp.where(key <= query, s, NEG)
    sbuf[0] = s
    top = jnp.max(s, axis=0, keepdims=True)

    def score(k, top):
        s = dot(kwin[rows_of(k), :], q, NT)
        sbuf[k] = s
        return jnp.maximum(top, jnp.max(s, axis=0, keepdims=True))

    top = lax.fori_loop(1, count, score, top) * factor

    def weigh(k, carry):
        total, along = carry
        e = jnp.exp2(sbuf[k] * factor - top)
        gp = dot(vwin[rows_of(k), :], g, NT)
        sbuf[k] = e
        gbuf[k] = gp
        total = total + jnp.sum(e, axis=0, keepdims=True)
        along = along + jnp.sum(e * gp, axis=0, keepdims=True)
        return total, along

    zero = jnp.zeros((1, lanes), jnp.float32)
    total, along = lax.fori_loop(0, count, weigh, (zero, zero))
    inverse = 1.0 / total
    along = along * inverse

    def finish(k, dqt):
        rows = rows_of(k)
        p = sbuf[k] * inverse
        ds = (p * (gbuf[k] - along)).astype(jnp.bfloat16)
        dk[rows, :] += dot(ds, q, NN)
        dv[rows, :] += dot(p.astype(jnp.bfloat16), g, NN)
        return dqt + dot(kwin[rows, :], ds, TN)

    dqt = lax.fori_loop(0, count, finish, jnp.zeros((head_dim, lanes), jnp.float32))
    dq = (dqt * scale).T.astype(jnp.bfloat16)
    dq_ref[...] = dq.reshape(group, BLK, head_dim)

    @pl.when(step == blocks_here - 1)
    def _():
        for offset in range(SPAN):
            rows = pl.ds((SPAN - 1 - offset) * tokens, tokens)
            target = own_ref if offset == 0 else far_refs[offset - 1]
            target[:, :head_dim] = (dk[rows, :] * scale).astype(target.dtype)
            target[:, head_dim:] = dv[rows, :].astype(target.dtype)


def attention(parents, pos, q, g, windows):
    group, tokens, head_dim = q.shape
    blocks_here = tokens // BLK
    lanes = group * BLK
    heads_block = pl.BlockSpec((group, BLK, head_dim), lambda i: (0, i, 0))
    whole = pl.BlockSpec((tokens, 2 * head_dim), lambda i: (0, 0))
    smem = pl.BlockSpec(memory_space=pltpu.SMEM)
    pair = lambda dtype: jax.ShapeDtypeStruct((tokens, 2 * head_dim), dtype)
    depth = SPAN * blocks_here
    return pl.pallas_call(
        functools.partial(
            attention_kernel,
            group=group,
            head_dim=head_dim,
            blocks_here=blocks_here,
            scale=1.0 / math.sqrt(head_dim),
        ),
        grid=(blocks_here,),
        in_specs=[smem, smem, heads_block, heads_block] + [whole] * SPAN,
        out_specs=[heads_block] + [whole] * SPAN,
        out_shape=[jax.ShapeDtypeStruct(q.shape, jnp.bfloat16), pair(jnp.float32)]
        + [pair(jnp.bfloat16)] * (SPAN - 1),
        scratch_shapes=[
            pltpu.VMEM((SPAN * tokens, head_dim), jnp.bfloat16),
            pltpu.VMEM((SPAN * tokens, head_dim), jnp.bfloat16),
            pltpu.VMEM((SPAN * tokens, head_dim), jnp.float32),
            pltpu.VMEM((SPAN * tokens, head_dim), jnp.float32),
            pltpu.VMEM((depth, BLK, lanes), jnp.float32),
            pltpu.VMEM((depth, BLK, lanes), jnp.float32),
            pltpu.SMEM((depth,), jnp.int32),
        ],
        compiler_params=pltpu.CompilerParams(
            dimension_semantics=("arbitrary",), vmem_limit_bytes=48 * 1024 * 1024
        ),
        cost_estimate=pl.CostEstimate(
            flops=20_000_000_000, bytes_accessed=8_000_000, transcendentals=0
        ),
        name="attention",
    )(parents, pos, q, g, *windows)


def project_kernel(me_ref, *refs, pieces, pairs):
    w_ref, out_ref, acc = refs[pieces * pairs :]
    step = pl.program_id(0)

    @pl.when(step == 0)
    def _():
        acc[...] = jnp.zeros_like(acc)

    w = w_ref[...]
    w = w.reshape(w.shape[0] * w.shape[2], w.shape[3])
    for index in range(pieces * pairs):

        @pl.when(step == index)
        def _():
            acc[...] += dot(refs[index][...], w, NN)

    @pl.when(step == pieces * pairs - 1)
    def _():
        out_ref[...] = acc[...].astype(jnp.bfloat16)


def project(me, grads, weights, pairs):
    pieces = len(grads) // pairs
    tokens = grads[0].shape[0]
    shards, _, rows, columns = weights.shape
    whole = pl.BlockSpec(grads[0].shape, lambda i, m: (0, 0))
    return pl.pallas_call(
        functools.partial(project_kernel, pieces=pieces, pairs=pairs),
        grid_spec=pltpu.PrefetchScalarGridSpec(
            num_scalar_prefetch=1,
            grid=(pieces * pairs,),
            in_specs=[whole] * len(grads)
            + [
                pl.BlockSpec(
                    (shards, 1, rows, columns),
                    lambda i, m: (0, (m[0] ^ (i % pieces)) * pairs + i // pieces, 0, 0),
                )
            ],
            out_specs=pl.BlockSpec((tokens, columns), lambda i, m: (0, 0)),
            scratch_shapes=[pltpu.VMEM((tokens, columns), jnp.float32)],
        ),
        out_shape=jax.ShapeDtypeStruct((tokens, columns), jnp.bfloat16),
        compiler_params=pltpu.CompilerParams(
            dimension_semantics=("arbitrary",), vmem_limit_bytes=48 * 1024 * 1024
        ),
        name="project",
    )(me, *grads, weights)


def body(queries, key_states, value_states, grad_output, parents, projection):
    tokens, heads, head_dim = queries.shape
    pairs = key_states.shape[1]
    group = heads // pairs
    seq_size = lax.axis_size("seq")
    fsdp_size = lax.axis_size("fsdp")
    pos = lax.axis_index("seq").astype(jnp.int32).reshape(1)
    me = lax.axis_index("fsdp").astype(jnp.int32).reshape(1)

    def shifted(x, by):
        steps = [(i, i + by) for i in range(seq_size)]
        steps = [(a, b) for a, b in steps if b >= 0 and a // SPAN == b // SPAN]
        return lax.ppermute(x, "seq", steps)

    windows = []
    for j in range(pairs):
        local = jnp.concatenate([key_states[:, j], value_states[:, j]], axis=1)
        windows.append([local] + [shifted(local, o) for o in range(1, SPAN)])

    rows = projection.shape[1]
    if rows % 16 == 0:
        weights = lax.all_gather(projection, "seq", axis=0)
    else:
        weights = lax.all_gather(projection, "seq", axis=1, tiled=True)[None]

    q = jnp.transpose(queries, (1, 0, 2))
    g = jnp.transpose(grad_output, (1, 0, 2))
    query_grads, pair_grads, gathered = [], [], []
    for j in range(pairs):
        mine = slice(j * group, (j + 1) * group)
        dq, own, *far = attention(parents, pos, q[mine], g[mine], windows[j])
        query_grads.append(dq)
        total = own
        for offset in range(1, SPAN):
            total = total + shifted(far[offset - 1], -offset).astype(jnp.float32)
        total = total.astype(jnp.bfloat16)
        pair_grads.append(total)
        pieces = [total]
        mask = 1
        while mask < fsdp_size:
            swap = [(i, i ^ mask) for i in range(fsdp_size)]
            pieces = pieces + [lax.ppermute(x, "fsdp", swap) for x in pieces]
            mask *= 2
        gathered += pieces

    grad_queries = jnp.transpose(jnp.concatenate(query_grads, axis=0), (1, 0, 2))
    grad_keys = jnp.stack([x[:, :head_dim] for x in pair_grads], axis=1)
    grad_values = jnp.stack([x[:, head_dim:] for x in pair_grads], axis=1)
    grad_inputs = project(me, gathered, weights, pairs)
    return (grad_queries, grad_keys, grad_values, grad_inputs)


def solution(mesh):
    in_specs = (
        P("seq", "fsdp", None),
        P("seq", "fsdp", None),
        P("seq", "fsdp", None),
        P("seq", "fsdp", None),
        P(),
        P(None, "seq", "fsdp"),
    )
    out_specs = (
        P("seq", "fsdp", None),
        P("seq", "fsdp", None),
        P("seq", "fsdp", None),
        P("seq", "fsdp"),
    )
    return jax.shard_map(body, mesh=mesh, in_specs=in_specs, out_specs=out_specs, check_vma=False)
```

```python
import functools
import math

import jax
import jax.numpy as jnp
from jax import lax
from jax.experimental import pallas as pl
from jax.experimental.pallas import tpu as pltpu
from jax.sharding import PartitionSpec as P

BLK = 128
SPAN = 4
NEG = -1e30
LOG2E = 1.4426950408889634

NT = (((1,), (1,)), ((), ()))
TN = (((0,), (0,)), ((), ()))
NN = (((1,), (0,)), ((), ()))


def dot(a, b, dims):
    return lax.dot_general(a, b, dims, preferred_element_type=jnp.float32)


def attention_kernel(parents_ref, pos_ref, q_ref, g_ref, *refs, group, head_dim, blocks_here, scale):
    kv_refs = refs[:SPAN]
    dq_ref, own_ref = refs[SPAN : SPAN + 2]
    far_refs = refs[SPAN + 2 : 2 * SPAN + 1]
    kwin, vwin, dk, dv, sbuf, gbuf, dq, path = refs[2 * SPAN + 1 :]
    step = pl.program_id(0)
    tokens = blocks_here * BLK
    lanes = group * BLK
    factor = scale * LOG2E

    @pl.when(step == 0)
    def _():
        for offset in range(SPAN):
            rows = pl.ds((SPAN - 1 - offset) * tokens, tokens)
            kwin[rows, :] = kv_refs[offset][:, :head_dim]
            vwin[rows, :] = kv_refs[offset][:, head_dim:]
        dk[...] = jnp.zeros_like(dk)
        dv[...] = jnp.zeros_like(dv)

    pos = pos_ref[0]
    first = (pos - (SPAN - 1)) * blocks_here
    lead = pos % SPAN
    stop = (pos - lead + 1) * blocks_here
    own = pos * blocks_here + step

    def walk(carry):
        current, count = carry
        path[count] = current - first
        return parents_ref[current], count + 1

    start = jnp.where(lead == 0, -1, own)
    path[1] = own - first
    count = lax.while_loop(lambda c: c[0] >= stop, walk, (start, jnp.int32(0)))[1]
    path[count] = own - first
    pairs = (count + 1) // 2

    def rows_of(k):
        return pl.ds(pl.multiple_of(path[k] * BLK, BLK), BLK)

    def pair_of(win, t):
        return jnp.concatenate([win[rows_of(2 * t), :], win[rows_of(2 * t + 1), :]], axis=0)

    def part(t):
        return pl.ds(pl.multiple_of(tokens + t * (2 * BLK), 2 * BLK), 2 * BLK)

    q = q_ref[...].reshape(lanes, head_dim)
    g = g_ref[...].reshape(lanes, head_dim)
    prompt = pl.ds(pl.multiple_of((SPAN - 1 - lead) * tokens, tokens), tokens)
    head = pl.ds(0, tokens)

    sbuf[head, :] = dot(kwin[prompt, :], q, NT)

    def score(t, _):
        sbuf[part(t), :] = dot(pair_of(kwin, t), q, NT)
        return 0

    lax.fori_loop(0, pairs, score, 0)

    @pl.when(lead == 0)
    def _():
        key = lax.broadcasted_iota(jnp.int32, (tokens, lanes), 0)
        query = lax.broadcasted_iota(jnp.int32, (tokens, lanes), 1) & (BLK - 1)
        sbuf[head, :] = jnp.where(key <= query + step * BLK, sbuf[head, :], NEG)

    @pl.when(lead > 0)
    def _():
        rows = pl.ds(tokens, BLK)
        key = lax.broadcasted_iota(jnp.int32, (BLK, lanes), 0)
        query = lax.broadcasted_iota(jnp.int32, (BLK, lanes), 1) & (BLK - 1)
        sbuf[rows, :] = jnp.where(key <= query, sbuf[rows, :], NEG)

    @pl.when(count < 2 * pairs)
    def _():
        rows = pl.ds(pl.multiple_of(tokens + count * BLK, BLK), BLK)
        sbuf[rows, :] = jnp.full((BLK, lanes), NEG, jnp.float32)

    top = jnp.max(sbuf[head, :], axis=0, keepdims=True)
    top = lax.fori_loop(
        0, pairs, lambda t, m: jnp.maximum(m, jnp.max(sbuf[part(t), :], axis=0, keepdims=True)), top
    )
    top = top * factor

    def weigh(rows, v, total, along):
        e = jnp.exp2(sbuf[rows, :] * factor - top)
        gp = dot(v, g, NT)
        sbuf[rows, :] = e
        gbuf[rows, :] = gp
        total = total + jnp.sum(e, axis=0, keepdims=True)
        along = along + jnp.sum(e * gp, axis=0, keepdims=True)
        return total, along

    zero = jnp.zeros((1, lanes), jnp.float32)
    carry = weigh(head, vwin[prompt, :], zero, zero)
    total, along = lax.fori_loop(
        0, pairs, lambda t, c: weigh(part(t), pair_of(vwin, t), *c), carry
    )
    inverse = 1.0 / total
    along = along * inverse

    def slopes(rows):
        p = sbuf[rows, :] * inverse
        ds = (p * (gbuf[rows, :] - along)).astype(jnp.bfloat16)
        return p.astype(jnp.bfloat16), ds

    p, ds = slopes(head)
    dk[prompt, :] += dot(ds, q, NN)
    dv[prompt, :] += dot(p, g, NN)
    dq[...] = dot(ds, kwin[prompt, :], TN)

    def finish(t, _):
        p, ds = slopes(part(t))
        dkt = dot(ds, q, NN)
        dvt = dot(p, g, NN)
        for half in range(2):
            rows = rows_of(2 * t + half)
            sub = slice(half * BLK, (half + 1) * BLK)
            dk[rows, :] += dkt[sub]
            dv[rows, :] += dvt[sub]
        dq[...] += dot(ds, pair_of(kwin, t), TN)
        return 0

    lax.fori_loop(0, pairs, finish, 0)
    dq_ref[...] = (dq[...] * scale).astype(jnp.bfloat16).reshape(group, BLK, head_dim)

    @pl.when(step == blocks_here - 1)
    def _():
        for offset in range(SPAN):
            rows = pl.ds((SPAN - 1 - offset) * tokens, tokens)
            target = own_ref if offset == 0 else far_refs[offset - 1]
            target[:, :head_dim] = (dk[rows, :] * scale).astype(target.dtype)
            target[:, head_dim:] = dv[rows, :].astype(target.dtype)


def attention(parents, pos, q, g, windows, j, group):
    _, tokens, head_dim = q.shape
    blocks_here = tokens // BLK
    lanes = group * BLK
    heads_block = pl.BlockSpec((group, BLK, head_dim), lambda i: (j, i, 0))
    dq_block = pl.BlockSpec((group, BLK, head_dim), lambda i: (0, i, 0))
    whole = pl.BlockSpec((tokens, 2 * head_dim), lambda i: (0, 0))
    smem = pl.BlockSpec(memory_space=pltpu.SMEM)
    pair = lambda dtype: jax.ShapeDtypeStruct((tokens, 2 * head_dim), dtype)
    depth = SPAN * blocks_here
    return pl.pallas_call(
        functools.partial(
            attention_kernel,
            group=group,
            head_dim=head_dim,
            blocks_here=blocks_here,
            scale=1.0 / math.sqrt(head_dim),
        ),
        grid=(blocks_here,),
        in_specs=[smem, smem, heads_block, heads_block] + [whole] * SPAN,
        out_specs=[dq_block] + [whole] * SPAN,
        out_shape=[jax.ShapeDtypeStruct((group, tokens, head_dim), jnp.bfloat16), pair(jnp.float32)] + [pair(jnp.bfloat16)] * (SPAN - 1),
        scratch_shapes=[
            pltpu.VMEM((SPAN * tokens, head_dim), jnp.bfloat16), pltpu.VMEM((SPAN * tokens, head_dim), jnp.bfloat16),
            pltpu.VMEM((SPAN * tokens, head_dim), jnp.float32), pltpu.VMEM((SPAN * tokens, head_dim), jnp.float32),
            pltpu.VMEM((depth * BLK, lanes), jnp.float32), pltpu.VMEM((depth * BLK, lanes), jnp.float32),
            pltpu.VMEM((lanes, head_dim), jnp.float32),
            pltpu.SMEM((depth + 1,), jnp.int32),
        ],
        compiler_params=pltpu.CompilerParams(dimension_semantics=("arbitrary",), vmem_limit_bytes=48 * 1024 * 1024),
        cost_estimate=pl.CostEstimate(flops=15_000_000_000, bytes_accessed=8_000_000, transcendentals=0),
        name="attention",
    )(parents, pos, q, g, *windows)


def project_kernel(place_ref, *refs, pieces, pairs, slots, wide):
    grads = refs[: pieces * pairs]
    shards = refs[pieces * pairs : pieces * pairs + slots]
    out_ref, wbuf, obuf, arrive, leave = refs[pieces * pairs + slots :]
    rows = shards[0].shape[1]
    blocks = wbuf.shape[0]

    def load(block, slot):
        target = pl.ds(pl.multiple_of(place_ref[1 + slot] * rows, rows), rows)
        return pltpu.make_async_copy(
            shards[slot].at[:, :, pl.ds(block * wide, wide)],
            wbuf.at[block, :, target, :],
            arrive.at[block, slot],
        )

    def store(block):
        part = pl.ds(block * wide, wide)
        return pltpu.make_async_copy(obuf.at[:, part], out_ref.at[:, part], leave.at[block])

    for block in range(blocks):
        for slot in range(slots):
            load(block, slot).start()
    me = place_ref[0]
    for block in range(blocks):
        for slot in range(slots):
            load(block, slot).wait()
        total = None
        for j in range(pairs):
            for piece in range(pieces):
                head = (me ^ piece) * pairs + j
                term = dot(grads[j * pieces + piece][...], wbuf[block, head], NN)
                total = term if total is None else total + term
        obuf[:, block * wide : (block + 1) * wide] = total.astype(jnp.bfloat16)
        store(block).start()
    for block in range(blocks):
        store(block).wait()


def project(place, grads, shards, pairs):
    pieces = len(grads) // pairs
    slots = len(shards)
    tokens = grads[0].shape[0]
    heads, rows, columns = shards[0].shape
    wide = 256 if columns % 256 == 0 else 128
    blocks = columns // wide
    vmem = pl.BlockSpec(memory_space=pltpu.VMEM)
    anywhere = pl.BlockSpec(memory_space=pl.ANY)
    return pl.pallas_call(
        functools.partial(project_kernel, pieces=pieces, pairs=pairs, slots=slots, wide=wide),
        in_specs=[pl.BlockSpec(memory_space=pltpu.SMEM)] + [vmem] * len(grads) + [anywhere] * slots,
        out_specs=anywhere,
        out_shape=jax.ShapeDtypeStruct((tokens, columns), jnp.bfloat16),
        scratch_shapes=[
            pltpu.VMEM((blocks, heads, slots * rows, wide), jnp.bfloat16),
            pltpu.VMEM((tokens, columns), jnp.bfloat16),
            pltpu.SemaphoreType.DMA((blocks, slots)),
            pltpu.SemaphoreType.DMA((blocks,)),
        ],
        compiler_params=pltpu.CompilerParams(vmem_limit_bytes=32 * 1024 * 1024),
        cost_estimate=pl.CostEstimate(
            flops=2_700_000_000, bytes_accessed=9_000_000, transcendentals=0
        ),
        name="project",
    )(place, *grads, *shards)


def ring_order(size):
    if size == 2 * SPAN:
        return list(range(0, size, 2)) + list(range(size - 1, 0, -2))
    return list(range(size))


def body(queries, key_states, value_states, grad_output, parents, projection):
    tokens, heads, head_dim = queries.shape
    pairs = key_states.shape[1]
    group = heads // pairs
    seq_size = lax.axis_size("seq")
    fsdp_size = lax.axis_size("fsdp")
    pos = lax.axis_index("seq").astype(jnp.int32).reshape(1)
    me = lax.axis_index("fsdp").astype(jnp.int32).reshape(1)

    def shifted(x, by):
        steps = [(i, i + by) for i in range(seq_size)]
        steps = [(a, b) for a, b in steps if b >= 0 and a // SPAN == b // SPAN]
        return lax.ppermute(x, "seq", steps)

    windows = []
    for j in range(pairs):
        local = jnp.concatenate([key_states[:, j], value_states[:, j]], axis=1)
        windows.append([local] + [shifted(local, o) for o in range(1, SPAN)])

    if projection.shape[1] % 16 == 0:
        order = ring_order(seq_size)
        ahead = [(order[c], order[(c + 1) % seq_size]) for c in range(seq_size)]
        behind = [(b, a) for a, b in ahead]
        rank_of = [order.index(s) for s in range(seq_size)]
        rank = jnp.asarray(rank_of, jnp.int32)[pos]
        shards, ranks = [projection], [rank]
        up = down = projection
        for k in range(1, (seq_size - 1) // 2 + 1):
            up = lax.ppermute(up, "seq", ahead)
            down = lax.ppermute(down, "seq", behind)
            shards += [up, down]
            ranks += [rank - k, rank + k]
        if seq_size % 2 == 0:
            half = projection.shape[0] // 2
            last_up = lax.ppermute(up[:half], "seq", ahead)
            last_down = lax.ppermute(down[half:], "seq", behind)
            shards.append(jnp.concatenate([last_up, last_down], axis=0))
            ranks.append(rank + seq_size // 2)
        places = jnp.asarray(order, jnp.int32)[jnp.concatenate(ranks) % seq_size]
    else:
        shards = [lax.all_gather(projection, "seq", axis=1, tiled=True)]
        places = jnp.zeros((1,), jnp.int32)

    q = jnp.transpose(queries, (1, 0, 2))
    g = jnp.transpose(grad_output, (1, 0, 2))
    query_grads, pair_grads, gathered = [], [], []
    for j in range(pairs):
        dq, own, *far = attention(parents, pos, q, g, windows[j], j, group)
        query_grads.append(dq)
        total = own
        for offset in range(1, SPAN):
            total = total + shifted(far[offset - 1], -offset).astype(jnp.float32)
        total = total.astype(jnp.bfloat16)
        pair_grads.append(total)
        pieces = [total]
        mask = 1
        while mask < fsdp_size:
            swap = [(i, i ^ mask) for i in range(fsdp_size)]
            pieces = pieces + [lax.ppermute(x, "fsdp", swap) for x in pieces]
            mask *= 2
        gathered += pieces

    grad_queries = jnp.transpose(jnp.concatenate(query_grads, axis=0), (1, 0, 2))
    grad_keys = jnp.stack([x[:, :head_dim] for x in pair_grads], axis=1)
    grad_values = jnp.stack([x[:, head_dim:] for x in pair_grads], axis=1)
    grad_inputs = project(jnp.concatenate([me, places]), gathered, shards, pairs)
    return (grad_queries, grad_keys, grad_values, grad_inputs)


def solution(mesh):
    in_specs = (
        P("seq", "fsdp", None),
        P("seq", "fsdp", None),
        P("seq", "fsdp", None),
        P("seq", "fsdp", None),
        P(),
        P(None, "seq", "fsdp"),
    )
    out_specs = (
        P("seq", "fsdp", None),
        P("seq", "fsdp", None),
        P("seq", "fsdp", None),
        P("seq", "fsdp"),
    )
    return jax.shard_map(body, mesh=mesh, in_specs=in_specs, out_specs=out_specs, check_vma=False)
```

```python
import functools
import math

import jax
import jax.numpy as jnp
from jax import lax
from jax.experimental import pallas as pl
from jax.experimental.pallas import tpu as pltpu
from jax.sharding import PartitionSpec as P

BLK = 128
SPAN = 4
NEG = -1e30
LOG2E = 1.4426950408889634

NT = (((1,), (1,)), ((), ()))
TN = (((0,), (0,)), ((), ()))
NN = (((1,), (0,)), ((), ()))


def dot(a, b, dims):
    return lax.dot_general(a, b, dims, preferred_element_type=jnp.float32)


def attention_kernel(
    parents_ref, q_ref, g_ref, *refs, group, head_dim, blocks_here, scale, j, last, waits, keeps
):
    kv_refs = refs[:SPAN]
    done_refs = refs[SPAN : SPAN + (j if last else 0)]
    refs = refs[:SPAN] + refs[SPAN + len(done_refs) + waits + keeps :]
    refs = refs[: 2 * SPAN + 1] + refs[2 * SPAN + 1 + keeps :]
    dq_ref, own_ref = refs[SPAN : SPAN + 2]
    far_refs = refs[SPAN + 2 : 2 * SPAN + 1]
    kwin, vwin, dk, dv, sbuf, gbuf, dq, path = refs[2 * SPAN + 1 :]
    step = pl.program_id(0)
    tokens = blocks_here * BLK
    lanes = group * BLK
    factor = scale * LOG2E

    @pl.when(step == 0)
    def _():
        for offset in range(SPAN):
            rows = pl.ds((SPAN - 1 - offset) * tokens, tokens)
            kwin[rows, :] = kv_refs[offset][:, :head_dim]
            vwin[rows, :] = kv_refs[offset][:, head_dim:]
        dk[...] = jnp.zeros_like(dk)
        dv[...] = jnp.zeros_like(dv)

    pos = lax.axis_index("seq")
    first = (pos - (SPAN - 1)) * blocks_here
    lead = pos % SPAN
    stop = (pos - lead + 1) * blocks_here
    own = pos * blocks_here + step

    def walk(carry):
        current, count = carry
        path[count] = current - first
        return parents_ref[current], count + 1

    start = jnp.where(lead == 0, -1, own)
    path[1] = own - first
    count = lax.while_loop(lambda c: c[0] >= stop, walk, (start, jnp.int32(0)))[1]
    path[count] = own - first
    pairs = (count + 1) // 2

    def rows_of(k):
        return pl.ds(pl.multiple_of(path[k] * BLK, BLK), BLK)

    def pair_of(win, t):
        return jnp.concatenate([win[rows_of(2 * t), :], win[rows_of(2 * t + 1), :]], axis=0)

    def part(t):
        return pl.ds(pl.multiple_of(tokens + t * (2 * BLK), 2 * BLK), 2 * BLK)

    def heads_of(ref):
        mine = ref[...].astype(jnp.float32)[:, j * group : (j + 1) * group, :]
        return mine.reshape(lanes, head_dim).astype(jnp.bfloat16)

    q = heads_of(q_ref)
    g = heads_of(g_ref)
    prompt = pl.ds(pl.multiple_of((SPAN - 1 - lead) * tokens, tokens), tokens)
    head = pl.ds(0, tokens)

    sbuf[head, :] = dot(kwin[prompt, :], q, NT)

    def score(t, _):
        sbuf[part(t), :] = dot(pair_of(kwin, t), q, NT)
        return 0

    lax.fori_loop(0, pairs, score, 0)

    @pl.when(lead == 0)
    def _():
        key = lax.broadcasted_iota(jnp.int32, (tokens, lanes), 0)
        query = lax.broadcasted_iota(jnp.int32, (tokens, lanes), 1) // group
        sbuf[head, :] = jnp.where(key <= query + step * BLK, sbuf[head, :], NEG)

    @pl.when(lead > 0)
    def _():
        rows = pl.ds(tokens, BLK)
        key = lax.broadcasted_iota(jnp.int32, (BLK, lanes), 0)
        query = lax.broadcasted_iota(jnp.int32, (BLK, lanes), 1) // group
        sbuf[rows, :] = jnp.where(key <= query, sbuf[rows, :], NEG)

    @pl.when(count < 2 * pairs)
    def _():
        rows = pl.ds(pl.multiple_of(tokens + count * BLK, BLK), BLK)
        sbuf[rows, :] = jnp.full((BLK, lanes), NEG, jnp.float32)

    top = jnp.max(sbuf[head, :], axis=0, keepdims=True)
    top = lax.fori_loop(
        0, pairs, lambda t, m: jnp.maximum(m, jnp.max(sbuf[part(t), :], axis=0, keepdims=True)), top
    )
    top = top * factor

    def weigh(rows, v, total, along):
        e = jnp.exp2(sbuf[rows, :] * factor - top)
        gp = dot(v, g, NT)
        sbuf[rows, :] = e
        gbuf[rows, :] = gp
        total = total + jnp.sum(e, axis=0, keepdims=True)
        along = along + jnp.sum(e * gp, axis=0, keepdims=True)
        return total, along

    zero = jnp.zeros((1, lanes), jnp.float32)
    carry = weigh(head, vwin[prompt, :], zero, zero)
    total, along = lax.fori_loop(
        0, pairs, lambda t, c: weigh(part(t), pair_of(vwin, t), *c), carry
    )
    inverse = 1.0 / total
    along = along * inverse

    def slopes(rows):
        p = sbuf[rows, :] * inverse
        ds = (p * (gbuf[rows, :] - along)).astype(jnp.bfloat16)
        return p.astype(jnp.bfloat16), ds

    p, ds = slopes(head)
    dk[prompt, :] += dot(ds, q, NN)
    dv[prompt, :] += dot(p, g, NN)
    dq[...] = dot(ds, kwin[prompt, :], TN)

    def finish(t, _):
        p, ds = slopes(part(t))
        dkt = dot(ds, q, NN)
        dvt = dot(p, g, NN)
        for half in range(2):
            rows = rows_of(2 * t + half)
            sub = slice(half * BLK, (half + 1) * BLK)
            dk[rows, :] += dkt[sub]
            dv[rows, :] += dvt[sub]
        dq[...] += dot(ds, pair_of(kwin, t), TN)
        return 0

    lax.fori_loop(0, pairs, finish, 0)
    mine = (dq[...] * scale).reshape(BLK, group, head_dim)
    if last:
        mine = jnp.concatenate([ref[...] for ref in done_refs] + [mine], axis=1)
    dq_ref[...] = mine.astype(dq_ref.dtype)

    @pl.when(step == blocks_here - 1)
    def _():
        for offset in range(SPAN):
            rows = pl.ds((SPAN - 1 - offset) * tokens, tokens)
            target = own_ref if offset == 0 else far_refs[offset - 1]
            target[:, :head_dim] = (dk[rows, :] * scale).astype(target.dtype)
            target[:, head_dim:] = dv[rows, :].astype(target.dtype)


def attention(parents, q, g, windows, j, pairs, done=(), waits=(), keeps=()):
    tokens, heads, head_dim = q.shape
    group = heads // pairs
    last = j == pairs - 1
    done = tuple(done) if last else ()
    blocks_here = tokens // BLK
    lanes = group * BLK
    depth = SPAN * blocks_here
    all_heads = pl.BlockSpec((BLK, heads, head_dim), lambda i: (i, 0, 0))
    some_heads = pl.BlockSpec((BLK, group, head_dim), lambda i: (i, 0, 0))
    whole = pl.BlockSpec((tokens, 2 * head_dim), lambda i: (0, 0))
    smem = pl.BlockSpec(memory_space=pltpu.SMEM)
    anywhere = pl.BlockSpec(memory_space=pl.ANY)
    pair = lambda dtype: jax.ShapeDtypeStruct((tokens, 2 * head_dim), dtype)
    if last:
        dq_shape = jax.ShapeDtypeStruct(q.shape, jnp.bfloat16)
    else:
        dq_shape = jax.ShapeDtypeStruct((tokens, group, head_dim), jnp.float32)
    return pl.pallas_call(
        functools.partial(
            attention_kernel,
            group=group,
            head_dim=head_dim,
            blocks_here=blocks_here,
            scale=1.0 / math.sqrt(head_dim),
            j=j,
            last=last,
            waits=len(waits),
            keeps=len(keeps),
        ),
        grid=(blocks_here,),
        in_specs=[smem, all_heads, all_heads]
        + [whole] * SPAN
        + [some_heads] * len(done)
        + [anywhere] * (len(waits) + len(keeps)),
        out_specs=[all_heads if last else some_heads] + [whole] * SPAN + [anywhere] * len(keeps),
        out_shape=[dq_shape, pair(jnp.float32)]
        + [pair(jnp.bfloat16)] * (SPAN - 1)
        + [jax.ShapeDtypeStruct(x.shape, x.dtype) for x in keeps],
        input_output_aliases={
            3 + SPAN + len(done) + len(waits) + i: 1 + SPAN + i for i in range(len(keeps))
        },
        scratch_shapes=[
            pltpu.VMEM((SPAN * tokens, head_dim), jnp.bfloat16),
            pltpu.VMEM((SPAN * tokens, head_dim), jnp.bfloat16),
            pltpu.VMEM((SPAN * tokens, head_dim), jnp.float32),
            pltpu.VMEM((SPAN * tokens, head_dim), jnp.float32),
            pltpu.VMEM((depth * BLK, lanes), jnp.float32),
            pltpu.VMEM((depth * BLK, lanes), jnp.float32),
            pltpu.VMEM((lanes, head_dim), jnp.float32),
            pltpu.SMEM((depth + 1,), jnp.int32),
        ],
        compiler_params=pltpu.CompilerParams(
            dimension_semantics=("arbitrary",), vmem_limit_bytes=48 * 1024 * 1024
        ),
        cost_estimate=pl.CostEstimate(
            flops=15_000_000_000, bytes_accessed=8_000_000, transcendentals=0
        ),
        name="attention",
    )(parents, q, g, *windows, *done, *waits, *keeps)


def ring_index_static(rank, size):
    if size != 2 * SPAN:
        return rank
    return 2 * rank if rank < size // 2 else 2 * (size - 1 - rank) + 1


def ring_rank(index, size):
    if size != 2 * SPAN:
        return index
    return jnp.where(index % 2 == 0, index // 2, size - 1 - index // 2)


def ring_index(rank, size):
    rank = (rank + size) % size
    if size != 2 * SPAN:
        return rank
    return jnp.where(rank < size // 2, 2 * rank, 2 * (size - 1 - rank) + 1)


def project_kernel(*refs, pieces, pairs, steps, size, wide):
    slots = len(steps)
    grads = refs[:pieces]
    shards = refs[pieces : pieces + slots]
    out_ref, wbuf, obuf, arrive, leave = refs[pieces + slots :]
    depth = grads[0].shape[1] // pairs
    rows = shards[0].shape[1]
    blocks = wbuf.shape[0]
    rank = ring_rank(lax.axis_index("seq"), size)
    me = lax.axis_index("fsdp")

    def load(block, slot):
        home = ring_index(rank + steps[slot], size) if slots > 1 else 0
        target = pl.ds(pl.multiple_of(home * rows, rows), rows)
        return pltpu.make_async_copy(
            shards[slot].at[:, :, pl.ds(block * wide, wide)],
            wbuf.at[block, :, target, :],
            arrive.at[block, slot],
        )

    def store(block):
        part = pl.ds(block * wide, wide)
        return pltpu.make_async_copy(obuf.at[:, part], out_ref.at[:, part], leave.at[block])

    for block in range(blocks):
        for slot in range(slots):
            load(block, slot).start()
    for block in range(blocks):
        for slot in range(slots):
            load(block, slot).wait()
        total = None
        for j in range(pairs):
            for piece in range(pieces):
                head = (me ^ piece) * pairs + j
                term = dot(grads[piece][:, j * depth : (j + 1) * depth], wbuf[block, head], NN)
                total = term if total is None else total + term
        obuf[:, block * wide : (block + 1) * wide] = total.astype(jnp.bfloat16)
        store(block).start()
    for block in range(blocks):
        store(block).wait()


def project(grads, shards, steps, pairs, size):
    pieces = len(grads)
    slots = len(shards)
    tokens = grads[0].shape[0]
    heads, rows, columns = shards[0].shape
    wide = 256 if columns % 256 == 0 else 128
    blocks = columns // wide
    vmem = pl.BlockSpec(memory_space=pltpu.VMEM)
    anywhere = pl.BlockSpec(memory_space=pl.ANY)
    return pl.pallas_call(
        functools.partial(
            project_kernel, pieces=pieces, pairs=pairs, steps=steps, size=size, wide=wide
        ),
        in_specs=[vmem] * len(grads) + [anywhere] * slots,
        out_specs=anywhere,
        out_shape=jax.ShapeDtypeStruct((tokens, columns), jnp.bfloat16),
        scratch_shapes=[
            pltpu.VMEM((blocks, heads, slots * rows, wide), jnp.bfloat16),
            pltpu.VMEM((tokens, columns), jnp.bfloat16),
            pltpu.SemaphoreType.DMA((blocks, slots)),
            pltpu.SemaphoreType.DMA((blocks,)),
        ],
        compiler_params=pltpu.CompilerParams(vmem_limit_bytes=32 * 1024 * 1024),
        cost_estimate=pl.CostEstimate(
            flops=2_700_000_000, bytes_accessed=9_000_000, transcendentals=0
        ),
        name="project",
    )(*grads, *shards)


def body(queries, key_states, value_states, grad_output, parents, projection):
    tokens, heads, head_dim = queries.shape
    pairs = key_states.shape[1]
    seq_size = lax.axis_size("seq")
    fsdp_size = lax.axis_size("fsdp")

    def shifted(x, by):
        moves = [(i, i + by) for i in range(seq_size)]
        moves = [(a, b) for a, b in moves if b >= 0 and a // SPAN == b // SPAN]
        return lax.ppermute(x, "seq", moves)

    order = [int(ring_index_static(c, seq_size)) for c in range(seq_size)]
    ahead = [(order[c], order[(c + 1) % seq_size]) for c in range(seq_size)]
    behind = [(b, a) for a, b in ahead]
    ring = projection.shape[1] % 16 == 0 and seq_size % 2 == 0
    shards, steps = [projection], [0]
    ends = (projection, projection)

    def ring_step(ends):
        distance = len(shards) // 2 + 1
        up, down = ends
        if 2 * distance < seq_size:
            up, down = lax.ppermute(up, "seq", ahead), lax.ppermute(down, "seq", behind)
            shards.extend([up, down])
            steps.extend([-distance, distance])
        else:
            half = projection.shape[0] // 2
            up = lax.ppermute(up[:half], "seq", ahead)
            down = lax.ppermute(down[half:], "seq", behind)
            shards.append(jnp.concatenate([up, down], axis=0))
            steps.append(distance)
        return up, down

    windows = []
    for j in range(pairs):
        local = jnp.concatenate([key_states[:, j], value_states[:, j]], axis=1)
        windows.append([local] + [shifted(local, o) for o in range(1, SPAN)])

    done, owns, returned, waits = [], [], [], ()
    for j in range(pairs):
        if ring:
            ends = ring_step(ends)
        dq, own, *rest = attention(
            parents, queries, grad_output, windows[j], j, pairs, done, waits, owns
        )
        waits = ends if ring else ()
        far, owns = rest[: SPAN - 1], rest[SPAN - 1 :] + [own]
        done.append(dq)
        returned.append([shifted(far[o - 1], -o) for o in range(1, SPAN)])
    grad_queries = done[-1]
    pair_grads = []
    for j in range(pairs):
        total = owns[j]
        for part in returned[j]:
            total = total + part.astype(jnp.float32)
        pair_grads.append(total.astype(jnp.bfloat16))
    gathered = [jnp.concatenate(pair_grads, axis=1)]
    mask = fsdp_size // 2
    while mask:
        swap = [(i, i ^ mask) for i in range(fsdp_size)]
        gathered = [y for x in gathered for y in (x, lax.ppermute(x, "fsdp", swap))]
        mask //= 2
    if ring:
        while len(shards) < seq_size:
            ends = ring_step(ends)
    else:
        shards, steps = [lax.all_gather(projection, "seq", axis=1, tiled=True)], [0]

    grad_keys = jnp.stack([x[:, :head_dim] for x in pair_grads], axis=1)
    grad_values = jnp.stack([x[:, head_dim:] for x in pair_grads], axis=1)
    grad_inputs = project(gathered, shards, tuple(steps), pairs, seq_size)
    return (grad_queries, grad_keys, grad_values, grad_inputs)


def solution(mesh):
    in_specs = (
        P("seq", "fsdp", None),
        P("seq", "fsdp", None),
        P("seq", "fsdp", None),
        P("seq", "fsdp", None),
        P(),
        P(None, "seq", "fsdp"),
    )
    out_specs = (
        P("seq", "fsdp", None),
        P("seq", "fsdp", None),
        P("seq", "fsdp", None),
        P("seq", "fsdp"),
    )
    return jax.shard_map(body, mesh=mesh, in_specs=in_specs, out_specs=out_specs, check_vma=False)
```

```python
import functools
import math

import jax
import jax.numpy as jnp
from jax import lax
from jax.experimental import pallas as pl
from jax.experimental.pallas import tpu as pltpu
from jax.sharding import PartitionSpec as P

BLK = 128
SPAN = 4
NEG = -1e30
LOG2E = 1.4426950408889634
SMALL = 2.0**-60
LARGE = 2.0**60
UNROLL = 3

NT = (((1,), (1,)), ((), ()))
TN = (((0,), (0,)), ((), ()))
NN = (((1,), (0,)), ((), ()))


def dot(a, b, dims):
    return lax.dot_general(a, b, dims, preferred_element_type=jnp.float32)


def attention_kernel(
    parents_ref, q_ref, g_ref, *refs, group, head_dim, blocks_here, scale, j, last, waits, keeps
):
    kv_refs = refs[:SPAN]
    done_refs = refs[SPAN : SPAN + (j if last else 0)]
    refs = refs[:SPAN] + refs[SPAN + len(done_refs) + waits + keeps :]
    refs = refs[: 2 * SPAN + 1] + refs[2 * SPAN + 1 + keeps :]
    dq_ref, own_ref = refs[SPAN : SPAN + 2]
    far_refs = refs[SPAN + 2 : 2 * SPAN + 1]
    kwin, vwin, kflip, dk, dv, ebuf, gbuf, path, total, along, dqt = refs[2 * SPAN + 1 :]
    step = pl.program_id(0)
    tokens = blocks_here * BLK
    lanes = group * BLK
    factor = scale * LOG2E

    @pl.when(step == 0)
    def _():
        for offset in range(SPAN):
            rows = pl.ds((SPAN - 1 - offset) * tokens, tokens)
            kwin[rows, :] = kv_refs[offset][:, :head_dim]
            vwin[rows, :] = kv_refs[offset][:, head_dim:]
            kflip[:, rows] = kv_refs[offset][:, :head_dim].T
        dk[...] = jnp.zeros_like(dk)
        dv[...] = jnp.zeros_like(dv)

    pos = lax.axis_index("seq")
    first = (pos - (SPAN - 1)) * blocks_here
    lead = pos % SPAN
    stop = (pos - lead + 1) * blocks_here
    own = pos * blocks_here + step

    def walk(carry):
        current, count = carry
        path[count] = current - first
        return parents_ref[current], count + 1

    start = jnp.where(lead == 0, -1, own)
    path[1] = own - first
    count = lax.while_loop(lambda c: c[0] >= stop, walk, (start, jnp.int32(0)))[1]
    path[count] = own - first
    pairs = (count + 1) // 2

    def rows_of(k):
        return pl.ds(pl.multiple_of(path[k] * BLK, BLK), BLK)

    def pair_of(win, t):
        return jnp.concatenate([win[rows_of(2 * t), :], win[rows_of(2 * t + 1), :]], axis=0)

    def part(t):
        return pl.ds(pl.multiple_of(tokens + t * (2 * BLK), 2 * BLK), 2 * BLK)

    def heads_of(ref):
        mine = ref[...].astype(jnp.float32)[:, j * group : (j + 1) * group, :]
        return mine.reshape(lanes, head_dim)

    q_wide = heads_of(q_ref)
    g_wide = heads_of(g_ref)
    q = q_wide.astype(jnp.bfloat16)
    g = g_wide.astype(jnp.bfloat16)
    prompt = pl.ds(pl.multiple_of((SPAN - 1 - lead) * tokens, tokens), tokens)
    head = pl.ds(0, tokens)
    query = lax.broadcasted_iota(jnp.int32, (1, lanes), 1) // group
    head_limit = query + jnp.where(lead == 0, step * BLK, tokens)

    def pair_visible(t):
        key = lax.broadcasted_iota(jnp.int32, (2 * BLK, lanes), 0)
        low = jnp.where(t == 0, query, BLK)
        high = jnp.where(2 * t + 1 < count, 2 * BLK, BLK - 1)
        return ((key <= low) & (key < BLK)) | ((key >= BLK) & (key <= high))

    def exponents(keys, visible, shift):
        s = dot(keys, q, NT) * factor
        if shift is not None:
            s = s - shift
        return s if visible is None else jnp.where(visible, s, NEG)

    def weigh(rows, keys, values, visible, shift, carry, fresh):
        e = jnp.exp2(exponents(keys, visible, shift))
        ebuf[rows, :] = e.astype(jnp.bfloat16)
        if fresh:
            gp = dot(values, g, NT)
            gbuf[rows, :] = gp
        else:
            gp = gbuf[rows, :]
        return (
            carry[0] + jnp.sum(e, axis=0, keepdims=True),
            carry[1] + jnp.sum(e * gp, axis=0, keepdims=True),
        )

    def head_visible():
        return lax.broadcasted_iota(jnp.int32, (tokens, lanes), 0) <= head_limit

    zero = jnp.zeros((1, lanes), jnp.float32)

    def gather(win, size):
        return jnp.concatenate(
            [win[prompt, :]] + [win[rows_of(k), :] for k in range(2 * size)], axis=0
        )

    def weigh_all(size):
        s = dot(gather(kwin, size), q, NT)
        gp = dot(gather(vwin, size), g, NT)
        gbuf[: tokens + 2 * size * BLK, :] = gp
        sums = (zero, zero)
        low = 0
        while low < tokens + 2 * size * BLK:
            high = tokens if low == 0 else low + BLK
            e = jnp.exp2(s[low:high] * factor)
            if low == 0 and size == 0:
                e = jnp.where(head_visible(), e, 0.0)
            if low == tokens:
                key = lax.broadcasted_iota(jnp.int32, (BLK, lanes), 0)
                e = jnp.where(key <= query, e, 0.0)
            elif low > 0 and high == tokens + 2 * size * BLK:
                e = jnp.where(count == 2 * size, e, 0.0)
            ebuf[low:high, :] = e.astype(jnp.bfloat16)
            sums = (
                sums[0] + jnp.sum(e, axis=0, keepdims=True),
                sums[1] + jnp.sum(e * gp[low:high], axis=0, keepdims=True),
            )
            low = high
        total[...], along[...] = sums

    def weigh_pair(t, carry, shift=None, fresh=True):
        return weigh(
            part(t), pair_of(kwin, t), pair_of(vwin, t), pair_visible(t), shift, carry, fresh
        )

    for size in range(UNROLL + 1):
        pl.when(pairs == size)(functools.partial(weigh_all, size))

    @pl.when(pairs > UNROLL)
    def _():
        carry = weigh(head, kwin[prompt, :], vwin[prompt, :], None, None, (zero, zero), True)
        total[...], along[...] = lax.fori_loop(0, pairs, weigh_pair, carry)

    @pl.when((jnp.min(total[...]) < SMALL) | ~(jnp.max(total[...]) < LARGE))
    def _():
        top = jnp.max(exponents(kwin[prompt, :], head_visible(), None), axis=0, keepdims=True)

        def highest(t, top):
            s = exponents(pair_of(kwin, t), pair_visible(t), None)
            return jnp.maximum(top, jnp.max(s, axis=0, keepdims=True))

        top = lax.fori_loop(0, pairs, highest, top)
        carry = weigh(head, kwin[prompt, :], None, head_visible(), top, (zero, zero), False)
        total[...], along[...] = lax.fori_loop(
            0, pairs, lambda t, c: weigh_pair(t, c, top, False), carry
        )

    inverse = 1.0 / total[...]
    mean = along[...] * inverse
    column = jnp.broadcast_to(inverse, (head_dim, lanes)).T
    q_scaled = (q_wide * column).astype(jnp.bfloat16)
    g_scaled = (g_wide * column).astype(jnp.bfloat16)

    def slopes(rows):
        e = ebuf[rows, :]
        return e, (e.astype(jnp.float32) * (gbuf[rows, :] - mean)).astype(jnp.bfloat16)

    def finish_all(size):
        e, ds = slopes(pl.ds(0, tokens + 2 * size * BLK))
        dkt = dot(ds, q_scaled, NN)
        dvt = dot(e, g_scaled, NN)
        dk[prompt, :] += dkt[:tokens]
        dv[prompt, :] += dvt[:tokens]
        for k in range(2 * size):
            rows = rows_of(k)
            sub = slice(tokens + k * BLK, tokens + (k + 1) * BLK)
            dk[rows, :] += dkt[sub]
            dv[rows, :] += dvt[sub]
        keys = [kflip[:, prompt]] + [kflip[:, rows_of(k)] for k in range(2 * size)]
        dqt[...] = dot(jnp.concatenate(keys, axis=1), ds, NN)

    for size in range(UNROLL + 1):
        pl.when(pairs == size)(functools.partial(finish_all, size))

    def finish(t, _):
        e, ds = slopes(part(t))
        dkt = dot(ds, q_scaled, NN)
        dvt = dot(e, g_scaled, NN)
        for half in range(2):
            rows = rows_of(2 * t + half)
            sub = slice(half * BLK, (half + 1) * BLK)
            dk[rows, :] += dkt[sub]
            dv[rows, :] += dvt[sub]
        keys = jnp.concatenate([kflip[:, rows_of(2 * t)], kflip[:, rows_of(2 * t + 1)]], axis=1)
        dqt[...] += dot(keys, ds, NN)
        return 0

    @pl.when(pairs > UNROLL)
    def _():
        finish_all(0)
        lax.fori_loop(0, pairs, finish, 0)

    mine = (dqt[...] * (inverse * scale)).T.reshape(BLK, group, head_dim)
    if last:
        mine = jnp.concatenate([ref[...] for ref in done_refs] + [mine], axis=1)
    dq_ref[...] = mine.astype(dq_ref.dtype)

    @pl.when(step == blocks_here - 1)
    def _():
        for offset in range(SPAN):
            rows = pl.ds((SPAN - 1 - offset) * tokens, tokens)
            target = own_ref if offset == 0 else far_refs[offset - 1]
            target[:, :head_dim] = (dk[rows, :] * scale).astype(target.dtype)
            target[:, head_dim:] = dv[rows, :].astype(target.dtype)


def attention(parents, q, g, windows, j, pairs, done=(), waits=(), keeps=()):
    tokens, heads, head_dim = q.shape
    group = heads // pairs
    last = j == pairs - 1
    done = tuple(done) if last else ()
    blocks_here = tokens // BLK
    lanes = group * BLK
    depth = SPAN * blocks_here
    all_heads = pl.BlockSpec((BLK, heads, head_dim), lambda i: (i, 0, 0))
    some_heads = pl.BlockSpec((BLK, group, head_dim), lambda i: (i, 0, 0))
    whole = pl.BlockSpec((tokens, 2 * head_dim), lambda i: (0, 0))
    smem = pl.BlockSpec(memory_space=pltpu.SMEM)
    anywhere = pl.BlockSpec(memory_space=pl.ANY)
    pair = lambda dtype: jax.ShapeDtypeStruct((tokens, 2 * head_dim), dtype)
    if last:
        dq_shape = jax.ShapeDtypeStruct(q.shape, jnp.bfloat16)
    else:
        dq_shape = jax.ShapeDtypeStruct((tokens, group, head_dim), jnp.float32)
    return pl.pallas_call(
        functools.partial(
            attention_kernel,
            group=group,
            head_dim=head_dim,
            blocks_here=blocks_here,
            scale=1.0 / math.sqrt(head_dim),
            j=j,
            last=last,
            waits=len(waits),
            keeps=len(keeps),
        ),
        grid=(blocks_here,),
        in_specs=[smem, all_heads, all_heads]
        + [whole] * SPAN
        + [some_heads] * len(done)
        + [anywhere] * (len(waits) + len(keeps)),
        out_specs=[all_heads if last else some_heads] + [whole] * SPAN + [anywhere] * len(keeps),
        out_shape=[dq_shape, pair(jnp.float32)]
        + [pair(jnp.bfloat16)] * (SPAN - 1)
        + [jax.ShapeDtypeStruct(x.shape, x.dtype) for x in keeps],
        input_output_aliases={
            3 + SPAN + len(done) + len(waits) + i: 1 + SPAN + i for i in range(len(keeps))
        },
        scratch_shapes=[
            pltpu.VMEM((SPAN * tokens, head_dim), jnp.bfloat16),
            pltpu.VMEM((SPAN * tokens, head_dim), jnp.bfloat16),
            pltpu.VMEM((head_dim, SPAN * tokens), jnp.bfloat16),
            pltpu.VMEM((SPAN * tokens, head_dim), jnp.float32),
            pltpu.VMEM((SPAN * tokens, head_dim), jnp.float32),
            pltpu.VMEM((depth * BLK, lanes), jnp.bfloat16),
            pltpu.VMEM((depth * BLK, lanes), jnp.float32),
            pltpu.SMEM((depth + 1,), jnp.int32),
            pltpu.VMEM((1, lanes), jnp.float32),
            pltpu.VMEM((1, lanes), jnp.float32),
            pltpu.VMEM((head_dim, lanes), jnp.float32),
        ],
        compiler_params=pltpu.CompilerParams(
            dimension_semantics=("arbitrary",), vmem_limit_bytes=48 * 1024 * 1024
        ),
        cost_estimate=pl.CostEstimate(
            flops=15_000_000_000, bytes_accessed=8_000_000, transcendentals=0
        ),
        name="attention",
    )(parents, q, g, *windows, *done, *waits, *keeps)


def ring_index_static(rank, size):
    if size != 2 * SPAN:
        return rank
    return 2 * rank if rank < size // 2 else 2 * (size - 1 - rank) + 1


def ring_rank(index, size):
    if size != 2 * SPAN:
        return index
    return jnp.where(index % 2 == 0, index // 2, size - 1 - index // 2)


def ring_index(rank, size):
    rank = (rank + size) % size
    if size != 2 * SPAN:
        return rank
    return jnp.where(rank < size // 2, 2 * rank, 2 * (size - 1 - rank) + 1)


def project_kernel(*refs, pieces, pairs, steps, size, wide):
    slots = len(steps)
    grads = refs[:pieces]
    shards = refs[pieces : pieces + slots]
    out_ref, wbuf, obuf, arrive, leave = refs[pieces + slots :]
    depth = grads[0].shape[1] // pairs
    rows = shards[0].shape[1]
    blocks = wbuf.shape[0]
    rank = ring_rank(lax.axis_index("seq"), size)
    me = lax.axis_index("fsdp")

    def load(block, slot):
        home = ring_index(rank + steps[slot], size) if slots > 1 else 0
        target = pl.ds(pl.multiple_of(home * rows, rows), rows)
        return pltpu.make_async_copy(
            shards[slot].at[:, :, pl.ds(block * wide, wide)],
            wbuf.at[block, :, target, :],
            arrive.at[block, slot],
        )

    def store(block):
        part = pl.ds(block * wide, wide)
        return pltpu.make_async_copy(obuf.at[:, part], out_ref.at[:, part], leave.at[block])

    for block in range(blocks):
        for slot in range(slots):
            load(block, slot).start()
    for block in range(blocks):
        for slot in range(slots):
            load(block, slot).wait()
        total = None
        for j in range(pairs):
            for piece in range(pieces):
                head = (me ^ piece) * pairs + j
                term = dot(grads[piece][:, j * depth : (j + 1) * depth], wbuf[block, head], NN)
                total = term if total is None else total + term
        obuf[:, block * wide : (block + 1) * wide] = total.astype(jnp.bfloat16)
        store(block).start()
    for block in range(blocks):
        store(block).wait()


def project(grads, shards, steps, pairs, size):
    pieces = len(grads)
    slots = len(shards)
    tokens = grads[0].shape[0]
    heads, rows, columns = shards[0].shape
    wide = 256 if columns % 256 == 0 else 128
    blocks = columns // wide
    vmem = pl.BlockSpec(memory_space=pltpu.VMEM)
    anywhere = pl.BlockSpec(memory_space=pl.ANY)
    return pl.pallas_call(
        functools.partial(
            project_kernel, pieces=pieces, pairs=pairs, steps=steps, size=size, wide=wide
        ),
        in_specs=[vmem] * len(grads) + [anywhere] * slots,
        out_specs=anywhere,
        out_shape=jax.ShapeDtypeStruct((tokens, columns), jnp.bfloat16),
        scratch_shapes=[
            pltpu.VMEM((blocks, heads, slots * rows, wide), jnp.bfloat16),
            pltpu.VMEM((tokens, columns), jnp.bfloat16),
            pltpu.SemaphoreType.DMA((blocks, slots)),
            pltpu.SemaphoreType.DMA((blocks,)),
        ],
        compiler_params=pltpu.CompilerParams(vmem_limit_bytes=32 * 1024 * 1024),
        cost_estimate=pl.CostEstimate(
            flops=2_700_000_000, bytes_accessed=9_000_000, transcendentals=0
        ),
        name="project",
    )(*grads, *shards)


def body(queries, key_states, value_states, grad_output, parents, projection):
    tokens, heads, head_dim = queries.shape
    pairs = key_states.shape[1]
    seq_size = lax.axis_size("seq")
    fsdp_size = lax.axis_size("fsdp")

    def shifted(x, by):
        moves = [(i, i + by) for i in range(seq_size)]
        moves = [(a, b) for a, b in moves if b >= 0 and a // SPAN == b // SPAN]
        return lax.ppermute(x, "seq", moves)

    order = [int(ring_index_static(c, seq_size)) for c in range(seq_size)]
    ahead = [(order[c], order[(c + 1) % seq_size]) for c in range(seq_size)]
    behind = [(b, a) for a, b in ahead]
    ring = projection.shape[1] % 16 == 0 and seq_size % 2 == 0
    shards, steps = [projection], [0]
    ends = (projection, projection)

    def ring_step(ends):
        distance = len(shards) // 2 + 1
        up, down = ends
        if 2 * distance < seq_size:
            up, down = lax.ppermute(up, "seq", ahead), lax.ppermute(down, "seq", behind)
            shards.extend([up, down])
            steps.extend([-distance, distance])
        else:
            half = projection.shape[0] // 2
            up = lax.ppermute(up[:half], "seq", ahead)
            down = lax.ppermute(down[half:], "seq", behind)
            shards.append(jnp.concatenate([up, down], axis=0))
            steps.append(distance)
        return up, down

    windows = []
    for j in range(pairs):
        local = jnp.concatenate([key_states[:, j], value_states[:, j]], axis=1)
        windows.append([local] + [shifted(local, o) for o in range(1, SPAN)])

    done, owns, returned, waits = [], [], [], ()
    for j in range(pairs):
        if ring:
            ends = ring_step(ends)
        dq, own, *rest = attention(
            parents, queries, grad_output, windows[j], j, pairs, done, waits, owns
        )
        waits = ends if ring else ()
        far, owns = rest[: SPAN - 1], rest[SPAN - 1 :] + [own]
        done.append(dq)
        returned.append([shifted(far[o - 1], -o) for o in range(1, SPAN)])
    grad_queries = done[-1]
    pair_grads = []
    for j in range(pairs):
        total = owns[j]
        for part in returned[j]:
            total = total + part.astype(jnp.float32)
        pair_grads.append(total.astype(jnp.bfloat16))
    gathered = [jnp.concatenate(pair_grads, axis=1)]
    mask = fsdp_size // 2
    while mask:
        swap = [(i, i ^ mask) for i in range(fsdp_size)]
        gathered = [y for x in gathered for y in (x, lax.ppermute(x, "fsdp", swap))]
        mask //= 2
    if ring:
        while len(shards) < seq_size:
            ends = ring_step(ends)
    else:
        shards, steps = [lax.all_gather(projection, "seq", axis=1, tiled=True)], [0]

    grad_keys = jnp.stack([x[:, :head_dim] for x in pair_grads], axis=1)
    grad_values = jnp.stack([x[:, head_dim:] for x in pair_grads], axis=1)
    grad_inputs = project(gathered, shards, tuple(steps), pairs, seq_size)
    return (grad_queries, grad_keys, grad_values, grad_inputs)


def solution(mesh):
    in_specs = (
        P("seq", "fsdp", None),
        P("seq", "fsdp", None),
        P("seq", "fsdp", None),
        P("seq", "fsdp", None),
        P(),
        P(None, "seq", "fsdp"),
    )
    out_specs = (
        P("seq", "fsdp", None),
        P("seq", "fsdp", None),
        P("seq", "fsdp", None),
        P("seq", "fsdp"),
    )
    return jax.shard_map(body, mesh=mesh, in_specs=in_specs, out_specs=out_specs, check_vma=False)
```

```python
import functools
import math

import jax
import jax.numpy as jnp
from jax import lax
from jax.experimental import pallas as pl
from jax.experimental.pallas import tpu as pltpu
from jax.sharding import PartitionSpec as P

BLK = 128
SPAN = 4
NEG = -1e30
LOG2E = 1.4426950408889634
SMALL = 2.0**-60
LARGE = 2.0**60
UNROLL = 2

NT = (((1,), (1,)), ((), ()))
TN = (((0,), (0,)), ((), ()))
NN = (((1,), (0,)), ((), ()))


def dot(a, b, dims):
    return lax.dot_general(a, b, dims, preferred_element_type=jnp.float32)


def attention_kernel(
    parents_ref, q_ref, g_ref, *refs, group, head_dim, blocks_here, scale, j, last, waits, keeps
):
    kv_refs = refs[:SPAN]
    done_refs = refs[SPAN : SPAN + (j if last else 0)]
    refs = refs[:SPAN] + refs[SPAN + len(done_refs) + waits + keeps :]
    refs = refs[: 2 * SPAN + 1] + refs[2 * SPAN + 1 + keeps :]
    dq_ref, own_ref = refs[SPAN : SPAN + 2]
    far_refs = refs[SPAN + 2 : 2 * SPAN + 1]
    kwin, vwin, kflip, dk, dv, ebuf, gbuf, path, total, along, dqt = refs[2 * SPAN + 1 :]
    step = pl.program_id(0)
    tokens = blocks_here * BLK
    lanes = group * BLK
    factor = scale * LOG2E

    @pl.when(step == 0)
    def _():
        for offset in range(SPAN):
            rows = pl.ds((SPAN - 1 - offset) * tokens, tokens)
            kwin[rows, :] = kv_refs[offset][:, :head_dim]
            vwin[rows, :] = kv_refs[offset][:, head_dim:]
            kflip[:, rows] = kv_refs[offset][:, :head_dim].T
        dk[...] = jnp.zeros_like(dk)
        dv[...] = jnp.zeros_like(dv)

    pos = lax.axis_index("seq")
    first = (pos - (SPAN - 1)) * blocks_here
    lead = pos % SPAN
    stop = (pos - lead + 1) * blocks_here
    own = pos * blocks_here + step

    def walk(carry):
        current, count = carry
        path[count] = current - first
        return parents_ref[current], count + 1

    start = jnp.where(lead == 0, -1, own)
    path[1] = own - first
    count = lax.while_loop(lambda c: c[0] >= stop, walk, (start, jnp.int32(0)))[1]
    path[count] = own - first
    pairs = (count + 1) // 2

    def rows_of(k):
        return pl.ds(pl.multiple_of(path[k] * BLK, BLK), BLK)

    def pair_of(win, t):
        return jnp.concatenate([win[rows_of(2 * t), :], win[rows_of(2 * t + 1), :]], axis=0)

    def part(t):
        return pl.ds(pl.multiple_of(tokens + t * (2 * BLK), 2 * BLK), 2 * BLK)

    def heads_of(ref):
        mine = ref[...].astype(jnp.float32)[:, j * group : (j + 1) * group, :]
        return mine.reshape(lanes, head_dim)

    q_wide = heads_of(q_ref)
    g_wide = heads_of(g_ref)
    q = q_wide.astype(jnp.bfloat16)
    g = g_wide.astype(jnp.bfloat16)
    prompt = pl.ds(pl.multiple_of((SPAN - 1 - lead) * tokens, tokens), tokens)
    head = pl.ds(0, tokens)
    query = lax.broadcasted_iota(jnp.int32, (1, lanes), 1) // group
    head_limit = query + jnp.where(lead == 0, step * BLK, tokens)

    def pair_visible(t):
        key = lax.broadcasted_iota(jnp.int32, (2 * BLK, lanes), 0)
        low = jnp.where(t == 0, query, BLK)
        high = jnp.where(2 * t + 1 < count, 2 * BLK, BLK - 1)
        return ((key <= low) & (key < BLK)) | ((key >= BLK) & (key <= high))

    def exponents(keys, visible, shift):
        s = dot(keys, q, NT) * factor
        if shift is not None:
            s = s - shift
        return s if visible is None else jnp.where(visible, s, NEG)

    def weigh(rows, keys, values, visible, shift, carry, fresh):
        e = jnp.exp2(exponents(keys, visible, shift))
        ebuf[rows, :] = e.astype(jnp.bfloat16)
        if fresh:
            gp = dot(values, g, NT)
            gbuf[rows, :] = gp
        else:
            gp = gbuf[rows, :]
        return (
            carry[0] + jnp.sum(e, axis=0, keepdims=True),
            carry[1] + jnp.sum(e * gp, axis=0, keepdims=True),
        )

    def head_visible():
        return lax.broadcasted_iota(jnp.int32, (tokens, lanes), 0) <= head_limit

    zero = jnp.zeros((1, lanes), jnp.float32)

    def gather(win, size):
        return jnp.concatenate(
            [win[prompt, :]] + [win[rows_of(k), :] for k in range(2 * size)], axis=0
        )

    def weigh_all(size):
        s = dot(gather(kwin, size), q, NT)
        gp = dot(gather(vwin, size), g, NT)
        gbuf[: tokens + 2 * size * BLK, :] = gp
        sums = (zero, zero)
        low = 0
        while low < tokens + 2 * size * BLK:
            high = tokens if low == 0 else low + BLK
            e = jnp.exp2(s[low:high] * factor)
            if low == tokens:
                key = lax.broadcasted_iota(jnp.int32, (BLK, lanes), 0)
                e = jnp.where(key <= query, e, 0.0)
            elif low > 0 and high == tokens + 2 * size * BLK:
                e = jnp.where(count == 2 * size, e, 0.0)
            ebuf[low:high, :] = e.astype(jnp.bfloat16)
            sums = (
                sums[0] + jnp.sum(e, axis=0, keepdims=True),
                sums[1] + jnp.sum(e * gp[low:high], axis=0, keepdims=True),
            )
            low = high
        total[...], along[...] = sums

    def weigh_pair(t, carry, shift=None, fresh=True):
        return weigh(
            part(t), pair_of(kwin, t), pair_of(vwin, t), pair_visible(t), shift, carry, fresh
        )

    for size in range(1, UNROLL + 1):
        pl.when(pairs == size)(functools.partial(weigh_all, size))

    @pl.when((pairs > UNROLL) | (pairs == 0))
    def _():
        carry = weigh(
            head, kwin[prompt, :], vwin[prompt, :], head_visible(), None, (zero, zero), True
        )
        total[...], along[...] = lax.fori_loop(0, pairs, weigh_pair, carry)

    @pl.when((jnp.min(total[...]) < SMALL) | ~(jnp.max(total[...]) < LARGE))
    def _():
        top = jnp.max(exponents(kwin[prompt, :], head_visible(), None), axis=0, keepdims=True)

        def highest(t, top):
            s = exponents(pair_of(kwin, t), pair_visible(t), None)
            return jnp.maximum(top, jnp.max(s, axis=0, keepdims=True))

        top = lax.fori_loop(0, pairs, highest, top)
        carry = weigh(head, kwin[prompt, :], None, head_visible(), top, (zero, zero), False)
        total[...], along[...] = lax.fori_loop(
            0, pairs, lambda t, c: weigh_pair(t, c, top, False), carry
        )

    inverse = 1.0 / total[...]
    mean = along[...] * inverse
    column = jnp.broadcast_to(inverse, (head_dim, lanes)).T
    q_scaled = (q_wide * column).astype(jnp.bfloat16)
    g_scaled = (g_wide * column).astype(jnp.bfloat16)

    def slopes(rows):
        e = ebuf[rows, :]
        return e, (e.astype(jnp.float32) * (gbuf[rows, :] - mean)).astype(jnp.bfloat16)

    def finish_all(size):
        e, ds = slopes(pl.ds(0, tokens + 2 * size * BLK))
        dkt = dot(ds, q_scaled, NN)
        dvt = dot(e, g_scaled, NN)
        dk[prompt, :] += dkt[:tokens]
        dv[prompt, :] += dvt[:tokens]
        for k in range(2 * size):
            rows = rows_of(k)
            sub = slice(tokens + k * BLK, tokens + (k + 1) * BLK)
            dk[rows, :] += dkt[sub]
            dv[rows, :] += dvt[sub]
        keys = [kflip[:, prompt]] + [kflip[:, rows_of(k)] for k in range(2 * size)]
        dqt[...] = dot(jnp.concatenate(keys, axis=1), ds, NN)

    for size in range(1, UNROLL + 1):
        pl.when(pairs == size)(functools.partial(finish_all, size))

    def finish(t, _):
        e, ds = slopes(part(t))
        dkt = dot(ds, q_scaled, NN)
        dvt = dot(e, g_scaled, NN)
        for half in range(2):
            rows = rows_of(2 * t + half)
            sub = slice(half * BLK, (half + 1) * BLK)
            dk[rows, :] += dkt[sub]
            dv[rows, :] += dvt[sub]
        keys = jnp.concatenate([kflip[:, rows_of(2 * t)], kflip[:, rows_of(2 * t + 1)]], axis=1)
        dqt[...] += dot(keys, ds, NN)
        return 0

    @pl.when((pairs > UNROLL) | (pairs == 0))
    def _():
        finish_all(0)
        lax.fori_loop(0, pairs, finish, 0)

    mine = (dqt[...] * (inverse * scale)).T.reshape(BLK, group, head_dim)
    if last:
        mine = jnp.concatenate([ref[...].astype(jnp.float32) for ref in done_refs] + [mine], axis=1)
    dq_ref[...] = mine.astype(dq_ref.dtype)

    @pl.when(step == blocks_here - 1)
    def _():
        for offset in range(SPAN):
            rows = pl.ds((SPAN - 1 - offset) * tokens, tokens)
            target = own_ref if offset == 0 else far_refs[offset - 1]
            target[:, :head_dim] = (dk[rows, :] * scale).astype(target.dtype)
            target[:, head_dim:] = dv[rows, :].astype(target.dtype)


def attention(parents, q, g, windows, j, pairs, done=(), waits=(), keeps=()):
    tokens, heads, head_dim = q.shape
    group = heads // pairs
    last = j == pairs - 1
    done = tuple(done) if last else ()
    blocks_here = tokens // BLK
    lanes = group * BLK
    depth = SPAN * blocks_here
    all_heads = pl.BlockSpec((BLK, heads, head_dim), lambda i: (i, 0, 0))
    some_heads = pl.BlockSpec((BLK, group, head_dim), lambda i: (i, 0, 0))
    whole = pl.BlockSpec((tokens, 2 * head_dim), lambda i: (0, 0))
    smem = pl.BlockSpec(memory_space=pltpu.SMEM)
    anywhere = pl.BlockSpec(memory_space=pl.ANY)
    pair = lambda dtype: jax.ShapeDtypeStruct((tokens, 2 * head_dim), dtype)
    if last:
        dq_shape = jax.ShapeDtypeStruct(q.shape, jnp.bfloat16)
    else:
        dq_shape = jax.ShapeDtypeStruct((tokens, group, head_dim), jnp.bfloat16)
    return pl.pallas_call(
        functools.partial(
            attention_kernel,
            group=group,
            head_dim=head_dim,
            blocks_here=blocks_here,
            scale=1.0 / math.sqrt(head_dim),
            j=j,
            last=last,
            waits=len(waits),
            keeps=len(keeps),
        ),
        grid=(blocks_here,),
        in_specs=[smem, all_heads, all_heads]
        + [whole] * SPAN
        + [some_heads] * len(done)
        + [anywhere] * (len(waits) + len(keeps)),
        out_specs=[all_heads if last else some_heads] + [whole] * SPAN + [anywhere] * len(keeps),
        out_shape=[dq_shape, pair(jnp.float32)]
        + [pair(jnp.bfloat16)] * (SPAN - 1)
        + [jax.ShapeDtypeStruct(x.shape, x.dtype) for x in keeps],
        input_output_aliases={
            3 + SPAN + len(done) + len(waits) + i: 1 + SPAN + i for i in range(len(keeps))
        },
        scratch_shapes=[
            pltpu.VMEM((SPAN * tokens, head_dim), jnp.bfloat16),
            pltpu.VMEM((SPAN * tokens, head_dim), jnp.bfloat16),
            pltpu.VMEM((head_dim, SPAN * tokens), jnp.bfloat16),
            pltpu.VMEM((SPAN * tokens, head_dim), jnp.float32),
            pltpu.VMEM((SPAN * tokens, head_dim), jnp.float32),
            pltpu.VMEM((depth * BLK, lanes), jnp.bfloat16),
            pltpu.VMEM((depth * BLK, lanes), jnp.float32),
            pltpu.SMEM((depth + 1,), jnp.int32),
            pltpu.VMEM((1, lanes), jnp.float32),
            pltpu.VMEM((1, lanes), jnp.float32),
            pltpu.VMEM((head_dim, lanes), jnp.float32),
        ],
        compiler_params=pltpu.CompilerParams(
            dimension_semantics=("arbitrary",), vmem_limit_bytes=48 * 1024 * 1024
        ),
        cost_estimate=pl.CostEstimate(
            flops=15_000_000_000, bytes_accessed=8_000_000, transcendentals=0
        ),
        name="attention",
    )(parents, q, g, *windows, *done, *waits, *keeps)


def ring_index_static(rank, size):
    if size != 2 * SPAN:
        return rank
    return 2 * rank if rank < size // 2 else 2 * (size - 1 - rank) + 1


def ring_rank(index, size):
    if size != 2 * SPAN:
        return index
    return jnp.where(index % 2 == 0, index // 2, size - 1 - index // 2)


def ring_index(rank, size):
    rank = (rank + size) % size
    if size != 2 * SPAN:
        return rank
    return jnp.where(rank < size // 2, 2 * rank, 2 * (size - 1 - rank) + 1)


def project_kernel(*refs, pieces, pairs, places, size, wide):
    slots = len(places)
    grads = refs[:pieces]
    shards = refs[pieces : pieces + slots]
    out_ref, wbuf, obuf, arrive, leave = refs[pieces + slots :]
    depth = grads[0].shape[1] // pairs
    rows = shards[0].shape[1]
    blocks = wbuf.shape[2] // wide
    rank = ring_rank(lax.axis_index("seq"), size)
    me = lax.axis_index("fsdp")

    def load(slot):
        head, step = places[slot]
        home = ring_index(rank + step, size) if slots > 1 else 0
        target = pl.ds(pl.multiple_of(home * rows, rows), rows)
        heads = pl.ds(head, shards[slot].shape[0])
        return pltpu.make_async_copy(
            shards[slot], wbuf.at[heads, target, :], arrive.at[slot]
        )

    def store(block):
        part = pl.ds(block * wide, wide)
        return pltpu.make_async_copy(obuf.at[:, part], out_ref.at[:, part], leave.at[block])

    for slot in range(slots):
        load(slot).start()
    for slot in range(slots):
        load(slot).wait()
    for block in range(blocks):
        part = slice(block * wide, (block + 1) * wide)
        total = None
        for j in range(pairs):
            for piece in range(pieces):
                head = (me ^ piece) * pairs + j
                grad = grads[piece][:, j * depth : (j + 1) * depth]
                term = dot(grad, wbuf[head, :, part], NN)
                total = term if total is None else total + term
        obuf[:, part] = total.astype(jnp.bfloat16)
        store(block).start()
    for block in range(blocks):
        store(block).wait()


def project(grads, shards, places, pairs, size):
    pieces = len(grads)
    slots = len(shards)
    tokens = grads[0].shape[0]
    heads, rows, columns = shards[0].shape
    depth = grads[0].shape[1] // pairs
    wide = 256 if columns % 256 == 0 else 128
    blocks = columns // wide
    vmem = pl.BlockSpec(memory_space=pltpu.VMEM)
    anywhere = pl.BlockSpec(memory_space=pl.ANY)
    return pl.pallas_call(
        functools.partial(
            project_kernel, pieces=pieces, pairs=pairs, places=places, size=size, wide=wide
        ),
        in_specs=[vmem] * len(grads) + [anywhere] * slots,
        out_specs=anywhere,
        out_shape=jax.ShapeDtypeStruct((tokens, columns), jnp.bfloat16),
        scratch_shapes=[
            pltpu.VMEM((heads, depth, columns), jnp.bfloat16),
            pltpu.VMEM((tokens, columns), jnp.bfloat16),
            pltpu.SemaphoreType.DMA((slots,)),
            pltpu.SemaphoreType.DMA((blocks,)),
        ],
        compiler_params=pltpu.CompilerParams(vmem_limit_bytes=32 * 1024 * 1024),
        cost_estimate=pl.CostEstimate(
            flops=2_700_000_000, bytes_accessed=9_000_000, transcendentals=0
        ),
        name="project",
    )(*grads, *shards)


def body(queries, key_states, value_states, grad_output, parents, projection):
    tokens, heads, head_dim = queries.shape
    pairs = key_states.shape[1]
    seq_size = lax.axis_size("seq")
    fsdp_size = lax.axis_size("fsdp")

    def shifted(x, by):
        moves = [(i, i + by) for i in range(seq_size)]
        moves = [(a, b) for a, b in moves if b >= 0 and a // SPAN == b // SPAN]
        return lax.ppermute(x, "seq", moves)

    order = [int(ring_index_static(c, seq_size)) for c in range(seq_size)]
    ahead = [(order[c], order[(c + 1) % seq_size]) for c in range(seq_size)]
    behind = [(b, a) for a, b in ahead]
    ring = projection.shape[1] % 16 == 0 and seq_size % 2 == 0
    shards, places = [projection], [(0, 0)]
    ends = (projection, projection)

    def ring_step(ends):
        distance = len(shards) // 2 + 1
        up, down = ends
        if 2 * distance < seq_size:
            up, down = lax.ppermute(up, "seq", ahead), lax.ppermute(down, "seq", behind)
            shards.extend([up, down])
            places.extend([(0, -distance), (0, distance)])
        else:
            half = projection.shape[0] // 2
            up = lax.ppermute(up[:half], "seq", ahead)
            down = lax.ppermute(down[half:], "seq", behind)
            shards.append(jnp.concatenate([up, down], axis=0))
            places.append((0, distance))
        return up, down

    windows = []
    for j in range(pairs):
        local = jnp.concatenate([key_states[:, j], value_states[:, j]], axis=1)
        windows.append([local] + [shifted(local, o) for o in range(1, SPAN)])

    done, owns, returned, waits = [], [], [], ()
    for j in range(pairs):
        if ring:
            ends = ring_step(ends)
        dq, own, *rest = attention(
            parents, queries, grad_output, windows[j], j, pairs, done, waits, owns
        )
        waits = ends if ring else ()
        far, owns = rest[: SPAN - 1], rest[SPAN - 1 :] + [own]
        done.append(dq)
        returned.append([shifted(far[o - 1], -o) for o in range(1, SPAN)])
    grad_queries = done[-1]
    pair_grads = []
    for j in range(pairs):
        total = owns[j]
        for part in returned[j]:
            total = total + part.astype(jnp.float32)
        pair_grads.append(total.astype(jnp.bfloat16))
    gathered = [jnp.concatenate(pair_grads, axis=1)]
    mask = fsdp_size // 2
    while mask:
        swap = [(i, i ^ mask) for i in range(fsdp_size)]
        gathered = [y for x in gathered for y in (x, lax.ppermute(x, "fsdp", swap))]
        mask //= 2
    if ring:
        while len(shards) < seq_size:
            ends = ring_step(ends)
    else:
        shards, places = [lax.all_gather(projection, "seq", axis=1, tiled=True)], [(0, 0)]

    grad_keys = jnp.stack([x[:, :head_dim] for x in pair_grads], axis=1)
    grad_values = jnp.stack([x[:, head_dim:] for x in pair_grads], axis=1)
    grad_inputs = project(gathered, shards, tuple(places), pairs, seq_size)
    return (grad_queries, grad_keys, grad_values, grad_inputs)


def solution(mesh):
    in_specs = (
        P("seq", "fsdp", None),
        P("seq", "fsdp", None),
        P("seq", "fsdp", None),
        P("seq", "fsdp", None),
        P(),
        P(None, "seq", "fsdp"),
    )
    out_specs = (
        P("seq", "fsdp", None),
        P("seq", "fsdp", None),
        P("seq", "fsdp", None),
        P("seq", "fsdp"),
    )
    return jax.shard_map(body, mesh=mesh, in_specs=in_specs, out_specs=out_specs, check_vma=False)
```

```python
import functools
import math

import jax
import jax.numpy as jnp
from jax import lax
from jax.experimental import pallas as pl
from jax.experimental.pallas import tpu as pltpu
from jax.sharding import PartitionSpec as P

BLK = 128
SPAN = 4
NEG = -1e30
LOG2E = 1.4426950408889634
SMALL = 2.0**-60
LARGE = 2.0**60
UNROLL = 2

NT = (((1,), (1,)), ((), ()))
TN = (((0,), (0,)), ((), ()))
NN = (((1,), (0,)), ((), ()))


def dot(a, b, dims):
    return lax.dot_general(a, b, dims, preferred_element_type=jnp.float32)


def attention_kernel(
    parents_ref, q_ref, g_ref, *refs, group, head_dim, blocks_here, scale, j, last, waits, keeps
):
    kv_refs = refs[:SPAN]
    done_refs = refs[SPAN : SPAN + (j if last else 0)]
    refs = refs[:SPAN] + refs[SPAN + len(done_refs) + waits + keeps :]
    refs = refs[: 2 * SPAN + 1] + refs[2 * SPAN + 1 + keeps :]
    dq_ref, own_ref = refs[SPAN : SPAN + 2]
    far_refs = refs[SPAN + 2 : 2 * SPAN + 1]
    kwin, vwin, kflip, dk, dv, ebuf, gbuf, path, total, along, dqt = refs[2 * SPAN + 1 :]
    step = pl.program_id(0)
    tokens = blocks_here * BLK
    lanes = group * BLK
    factor = scale * LOG2E

    @pl.when(step == 0)
    def _():
        for offset in range(SPAN):
            rows = pl.ds((SPAN - 1 - offset) * tokens, tokens)
            kwin[rows, :] = kv_refs[offset][:, :head_dim]
            vwin[rows, :] = kv_refs[offset][:, head_dim:]
            kflip[:, rows] = kv_refs[offset][:, :head_dim].T
        dk[...] = jnp.zeros_like(dk)
        dv[...] = jnp.zeros_like(dv)

    pos = lax.axis_index("seq")
    first = (pos - (SPAN - 1)) * blocks_here
    lead = pos % SPAN
    stop = (pos - lead + 1) * blocks_here
    own = pos * blocks_here + step

    def walk(carry):
        current, count = carry
        path[count] = current - first
        return parents_ref[current], count + 1

    start = jnp.where(lead == 0, -1, own)
    path[1] = own - first
    count = lax.while_loop(lambda c: c[0] >= stop, walk, (start, jnp.int32(0)))[1]
    path[count] = own - first
    pairs = (count + 1) // 2

    def rows_of(k):
        return pl.ds(pl.multiple_of(path[k] * BLK, BLK), BLK)

    def pair_of(win, t):
        return jnp.concatenate([win[rows_of(2 * t), :], win[rows_of(2 * t + 1), :]], axis=0)

    def part(t):
        return pl.ds(pl.multiple_of(tokens + t * (2 * BLK), 2 * BLK), 2 * BLK)

    def heads_of(ref):
        mine = ref[...].astype(jnp.float32)[:, j * group : (j + 1) * group, :]
        return mine.reshape(lanes, head_dim)

    q_wide = heads_of(q_ref)
    g_wide = heads_of(g_ref)
    q = q_wide.astype(jnp.bfloat16)
    g = g_wide.astype(jnp.bfloat16)
    prompt = pl.ds(pl.multiple_of((SPAN - 1 - lead) * tokens, tokens), tokens)
    head = pl.ds(0, tokens)
    query = lax.broadcasted_iota(jnp.int32, (1, lanes), 1) // group
    head_limit = query + jnp.where(lead == 0, step * BLK, tokens)

    def pair_visible(t):
        key = lax.broadcasted_iota(jnp.int32, (2 * BLK, lanes), 0)
        low = jnp.where(t == 0, query, BLK)
        high = jnp.where(2 * t + 1 < count, 2 * BLK, BLK - 1)
        return ((key <= low) & (key < BLK)) | ((key >= BLK) & (key <= high))

    def exponents(keys, visible, shift):
        s = dot(keys, q, NT) * factor
        if shift is not None:
            s = s - shift
        return s if visible is None else jnp.where(visible, s, NEG)

    def weigh(rows, keys, values, visible, shift, carry, fresh):
        e = jnp.exp2(exponents(keys, visible, shift))
        ebuf[rows, :] = e.astype(jnp.bfloat16)
        if fresh:
            gp = dot(values, g, NT)
            gbuf[rows, :] = gp
        else:
            gp = gbuf[rows, :]
        return (
            carry[0] + jnp.sum(e, axis=0, keepdims=True),
            carry[1] + jnp.sum(e * gp, axis=0, keepdims=True),
        )

    def head_visible():
        return lax.broadcasted_iota(jnp.int32, (tokens, lanes), 0) <= head_limit

    zero = jnp.zeros((1, lanes), jnp.float32)

    def gather(win, size):
        return jnp.concatenate(
            [win[prompt, :]] + [win[rows_of(k), :] for k in range(2 * size)], axis=0
        )

    def weigh_all(size):
        s = dot(gather(kwin, size), q, NT)
        gp = dot(gather(vwin, size), g, NT)
        gbuf[: tokens + 2 * size * BLK, :] = gp
        sums = (zero, zero)
        low = 0
        while low < tokens + 2 * size * BLK:
            high = tokens if low == 0 else low + BLK
            e = jnp.exp2(s[low:high] * factor)
            if low == tokens:
                key = lax.broadcasted_iota(jnp.int32, (BLK, lanes), 0)
                e = jnp.where(key <= query, e, 0.0)
            elif low > 0 and high == tokens + 2 * size * BLK:
                e = jnp.where(count == 2 * size, e, 0.0)
            ebuf[low:high, :] = e.astype(jnp.bfloat16)
            sums = (
                sums[0] + jnp.sum(e, axis=0, keepdims=True),
                sums[1] + jnp.sum(e * gp[low:high], axis=0, keepdims=True),
            )
            low = high
        total[...], along[...] = sums

    def weigh_pair(t, carry, shift=None, fresh=True):
        return weigh(
            part(t), pair_of(kwin, t), pair_of(vwin, t), pair_visible(t), shift, carry, fresh
        )

    for size in range(1, UNROLL + 1):
        pl.when(pairs == size)(functools.partial(weigh_all, size))

    @pl.when((pairs > UNROLL) | (pairs == 0))
    def _():
        carry = weigh(
            head, kwin[prompt, :], vwin[prompt, :], head_visible(), None, (zero, zero), True
        )
        total[...], along[...] = lax.fori_loop(0, pairs, weigh_pair, carry)

    @pl.when((jnp.min(total[...]) < SMALL) | ~(jnp.max(total[...]) < LARGE))
    def _():
        top = jnp.max(exponents(kwin[prompt, :], head_visible(), None), axis=0, keepdims=True)

        def highest(t, top):
            s = exponents(pair_of(kwin, t), pair_visible(t), None)
            return jnp.maximum(top, jnp.max(s, axis=0, keepdims=True))

        top = lax.fori_loop(0, pairs, highest, top)
        carry = weigh(head, kwin[prompt, :], None, head_visible(), top, (zero, zero), False)
        total[...], along[...] = lax.fori_loop(
            0, pairs, lambda t, c: weigh_pair(t, c, top, False), carry
        )

    inverse = 1.0 / total[...]
    mean = along[...] * inverse
    column = jnp.broadcast_to(inverse, (head_dim, lanes)).T
    q_scaled = (q_wide * column).astype(jnp.bfloat16)
    g_scaled = (g_wide * column).astype(jnp.bfloat16)

    def slopes(rows):
        e = ebuf[rows, :]
        return e, (e.astype(jnp.float32) * (gbuf[rows, :] - mean)).astype(jnp.bfloat16)

    def finish_all(size):
        e, ds = slopes(pl.ds(0, tokens + 2 * size * BLK))
        dkt = dot(ds, q_scaled, NN)
        dvt = dot(e, g_scaled, NN)
        dk[prompt, :] += dkt[:tokens]
        dv[prompt, :] += dvt[:tokens]
        for k in range(2 * size):
            rows = rows_of(k)
            sub = slice(tokens + k * BLK, tokens + (k + 1) * BLK)
            dk[rows, :] += dkt[sub]
            dv[rows, :] += dvt[sub]
        keys = [kflip[:, prompt]] + [kflip[:, rows_of(k)] for k in range(2 * size)]
        dqt[...] = dot(jnp.concatenate(keys, axis=1), ds, NN)

    for size in range(1, UNROLL + 1):
        pl.when(pairs == size)(functools.partial(finish_all, size))

    def finish(t, _):
        e, ds = slopes(part(t))
        dkt = dot(ds, q_scaled, NN)
        dvt = dot(e, g_scaled, NN)
        for half in range(2):
            rows = rows_of(2 * t + half)
            sub = slice(half * BLK, (half + 1) * BLK)
            dk[rows, :] += dkt[sub]
            dv[rows, :] += dvt[sub]
        keys = jnp.concatenate([kflip[:, rows_of(2 * t)], kflip[:, rows_of(2 * t + 1)]], axis=1)
        dqt[...] += dot(keys, ds, NN)
        return 0

    @pl.when((pairs > UNROLL) | (pairs == 0))
    def _():
        finish_all(0)
        lax.fori_loop(0, pairs, finish, 0)

    mine = (dqt[...] * (inverse * scale)).T.reshape(BLK, group, head_dim)
    if last:
        mine = jnp.concatenate([ref[...].astype(jnp.float32) for ref in done_refs] + [mine], axis=1)
    dq_ref[...] = mine.astype(dq_ref.dtype)

    @pl.when(step == blocks_here - 1)
    def _():
        for offset in range(SPAN):
            rows = pl.ds((SPAN - 1 - offset) * tokens, tokens)
            target = own_ref if offset == 0 else far_refs[offset - 1]
            target[:, :head_dim] = (dk[rows, :] * scale).astype(target.dtype)
            target[:, head_dim:] = dv[rows, :].astype(target.dtype)


def attention(parents, q, g, windows, j, pairs, done=(), waits=(), keeps=()):
    tokens, heads, head_dim = q.shape
    group = heads // pairs
    last = j == pairs - 1
    done = tuple(done) if last else ()
    blocks_here = tokens // BLK
    lanes = group * BLK
    depth = SPAN * blocks_here
    all_heads = pl.BlockSpec((BLK, heads, head_dim), lambda i: (i, 0, 0))
    some_heads = pl.BlockSpec((BLK, group, head_dim), lambda i: (i, 0, 0))
    whole = pl.BlockSpec((tokens, 2 * head_dim), lambda i: (0, 0))
    smem = pl.BlockSpec(memory_space=pltpu.SMEM)
    anywhere = pl.BlockSpec(memory_space=pl.ANY)
    pair = lambda dtype: jax.ShapeDtypeStruct((tokens, 2 * head_dim), dtype)
    if last:
        dq_shape = jax.ShapeDtypeStruct(q.shape, jnp.bfloat16)
    else:
        dq_shape = jax.ShapeDtypeStruct((tokens, group, head_dim), jnp.bfloat16)
    return pl.pallas_call(
        functools.partial(
            attention_kernel,
            group=group,
            head_dim=head_dim,
            blocks_here=blocks_here,
            scale=1.0 / math.sqrt(head_dim),
            j=j,
            last=last,
            waits=len(waits),
            keeps=len(keeps),
        ),
        grid=(blocks_here,),
        in_specs=[smem, all_heads, all_heads]
        + [whole] * SPAN
        + [some_heads] * len(done)
        + [anywhere] * (len(waits) + len(keeps)),
        out_specs=[all_heads if last else some_heads] + [whole] * SPAN + [anywhere] * len(keeps),
        out_shape=[dq_shape, pair(jnp.float32)]
        + [pair(jnp.bfloat16)] * (SPAN - 1)
        + [jax.ShapeDtypeStruct(x.shape, x.dtype) for x in keeps],
        input_output_aliases={
            3 + SPAN + len(done) + len(waits) + i: 1 + SPAN + i for i in range(len(keeps))
        },
        scratch_shapes=[
            pltpu.VMEM((SPAN * tokens, head_dim), jnp.bfloat16),
            pltpu.VMEM((SPAN * tokens, head_dim), jnp.bfloat16),
            pltpu.VMEM((head_dim, SPAN * tokens), jnp.bfloat16),
            pltpu.VMEM((SPAN * tokens, head_dim), jnp.float32),
            pltpu.VMEM((SPAN * tokens, head_dim), jnp.float32),
            pltpu.VMEM((depth * BLK, lanes), jnp.bfloat16),
            pltpu.VMEM((depth * BLK, lanes), jnp.float32),
            pltpu.SMEM((depth + 1,), jnp.int32),
            pltpu.VMEM((1, lanes), jnp.float32),
            pltpu.VMEM((1, lanes), jnp.float32),
            pltpu.VMEM((head_dim, lanes), jnp.float32),
        ],
        compiler_params=pltpu.CompilerParams(
            dimension_semantics=("arbitrary",), vmem_limit_bytes=48 * 1024 * 1024
        ),
        cost_estimate=pl.CostEstimate(
            flops=15_000_000_000, bytes_accessed=8_000_000, transcendentals=0
        ),
        name="attention",
    )(parents, q, g, *windows, *done, *waits, *keeps)


def ring_index_static(rank, size):
    if size != 2 * SPAN:
        return rank
    return 2 * rank if rank < size // 2 else 2 * (size - 1 - rank) + 1


def ring_rank(index, size):
    if size != 2 * SPAN:
        return index
    return jnp.where(index % 2 == 0, index // 2, size - 1 - index // 2)


def ring_index(rank, size):
    rank = (rank + size) % size
    if size != 2 * SPAN:
        return rank
    return jnp.where(rank < size // 2, 2 * rank, 2 * (size - 1 - rank) + 1)


def project_kernel(*refs, pieces, pairs, places, size, wide):
    slots = len(places)
    grads = refs[:pieces]
    shards = refs[pieces : pieces + slots]
    out_ref, wbuf, obuf, arrive, leave = refs[pieces + slots :]
    depth = grads[0].shape[1] // pairs
    rows = shards[0].shape[1]
    blocks = wbuf.shape[2] // wide
    rank = ring_rank(lax.axis_index("seq"), size)
    me = lax.axis_index("fsdp")

    def load(slot):
        head, step = places[slot]
        home = ring_index(rank + step, size) if slots > 1 else 0
        target = pl.ds(pl.multiple_of(home * rows, rows), rows)
        heads = pl.ds(head, shards[slot].shape[0])
        return pltpu.make_async_copy(
            shards[slot], wbuf.at[heads, target, :], arrive.at[slot]
        )

    def store(block):
        part = pl.ds(block * wide, wide)
        return pltpu.make_async_copy(obuf.at[:, part], out_ref.at[:, part], leave.at[block])

    for slot in range(slots):
        load(slot).start()
    for slot in range(slots):
        load(slot).wait()
    for block in range(blocks):
        part = slice(block * wide, (block + 1) * wide)
        total = None
        for j in range(pairs):
            for piece in range(pieces):
                head = (me ^ piece) * pairs + j
                grad = grads[piece][:, j * depth : (j + 1) * depth]
                term = dot(grad, wbuf[head, :, part], NN)
                total = term if total is None else total + term
        obuf[:, part] = total.astype(jnp.bfloat16)
        store(block).start()
    for block in range(blocks):
        store(block).wait()


def project(grads, shards, places, pairs, size):
    pieces = len(grads)
    slots = len(shards)
    tokens = grads[0].shape[0]
    heads, rows, columns = shards[0].shape
    depth = grads[0].shape[1] // pairs
    wide = 256 if columns % 256 == 0 else 128
    blocks = columns // wide
    vmem = pl.BlockSpec(memory_space=pltpu.VMEM)
    anywhere = pl.BlockSpec(memory_space=pl.ANY)
    return pl.pallas_call(
        functools.partial(
            project_kernel, pieces=pieces, pairs=pairs, places=places, size=size, wide=wide
        ),
        in_specs=[vmem] * len(grads) + [anywhere] * slots,
        out_specs=anywhere,
        out_shape=jax.ShapeDtypeStruct((tokens, columns), jnp.bfloat16),
        scratch_shapes=[
            pltpu.VMEM((heads, depth, columns), jnp.bfloat16),
            pltpu.VMEM((tokens, columns), jnp.bfloat16),
            pltpu.SemaphoreType.DMA((slots,)),
            pltpu.SemaphoreType.DMA((blocks,)),
        ],
        compiler_params=pltpu.CompilerParams(vmem_limit_bytes=32 * 1024 * 1024),
        cost_estimate=pl.CostEstimate(
            flops=2_700_000_000, bytes_accessed=9_000_000, transcendentals=0
        ),
        name="project",
    )(*grads, *shards)


def body(queries, key_states, value_states, grad_output, parents, projection):
    tokens, heads, head_dim = queries.shape
    pairs = key_states.shape[1]
    seq_size = lax.axis_size("seq")
    fsdp_size = lax.axis_size("fsdp")

    def shifted(x, by):
        moves = [(i, i + by) for i in range(seq_size)]
        moves = [(a, b) for a, b in moves if b >= 0 and a // SPAN == b // SPAN]
        return lax.ppermute(x, "seq", moves)

    order = [int(ring_index_static(c, seq_size)) for c in range(seq_size)]
    ahead = [(order[c], order[(c + 1) % seq_size]) for c in range(seq_size)]
    behind = [(b, a) for a, b in ahead]
    ring = projection.shape[1] % 16 == 0 and seq_size % 2 == 0
    shards, places = [projection], [(0, 0)]
    ends = (projection, projection)

    def ring_step(ends):
        distance = len(shards) // 2 + 1
        up, down = ends
        if 2 * distance < seq_size:
            up, down = lax.ppermute(up, "seq", ahead), lax.ppermute(down, "seq", behind)
            shards.extend([up, down])
            places.extend([(0, -distance), (0, distance)])
        else:
            half = projection.shape[0] // 2
            up = lax.ppermute(up[:half], "seq", ahead)
            down = lax.ppermute(down[half:], "seq", behind)
            shards.append(jnp.concatenate([up, down], axis=0))
            places.append((0, distance))
        return up, down

    windows = []
    both = jnp.concatenate([key_states, value_states], axis=2)
    for j in range(pairs):
        local = both[:, j]
        windows.append([local] + [shifted(local, o) for o in range(1, SPAN)])

    done, owns, returned, waits = [], [], [], ()
    for j in range(pairs):
        if ring:
            ends = ring_step(ends)
        dq, own, *rest = attention(
            parents, queries, grad_output, windows[j], j, pairs, done, waits, owns
        )
        waits = ends if ring else ()
        far, owns = rest[: SPAN - 1], rest[SPAN - 1 :] + [own]
        done.append(dq)
        returned.append([shifted(far[o - 1], -o) for o in range(1, SPAN)])
    grad_queries = done[-1]
    pair_grads = []
    for j in range(pairs):
        total = owns[j]
        for part in returned[j]:
            total = total + part.astype(jnp.float32)
        pair_grads.append(total.astype(jnp.bfloat16))
    gathered = [jnp.concatenate(pair_grads, axis=1)]
    mask = fsdp_size // 2
    while mask:
        swap = [(i, i ^ mask) for i in range(fsdp_size)]
        gathered = [y for x in gathered for y in (x, lax.ppermute(x, "fsdp", swap))]
        mask //= 2
    if ring:
        while len(shards) < seq_size:
            ends = ring_step(ends)
    else:
        shards, places = [lax.all_gather(projection, "seq", axis=1, tiled=True)], [(0, 0)]

    grad_keys = jnp.stack([x[:, :head_dim] for x in pair_grads], axis=1)
    grad_values = jnp.stack([x[:, head_dim:] for x in pair_grads], axis=1)
    grad_inputs = project(gathered, shards, tuple(places), pairs, seq_size)
    return (grad_queries, grad_keys, grad_values, grad_inputs)


def solution(mesh):
    in_specs = (
        P("seq", "fsdp", None),
        P("seq", "fsdp", None),
        P("seq", "fsdp", None),
        P("seq", "fsdp", None),
        P(),
        P(None, "seq", "fsdp"),
    )
    out_specs = (
        P("seq", "fsdp", None),
        P("seq", "fsdp", None),
        P("seq", "fsdp", None),
        P("seq", "fsdp"),
    )
    return jax.shard_map(body, mesh=mesh, in_specs=in_specs, out_specs=out_specs, check_vma=False)
```
